128 devices in a mesh: gx: 16 (over z, y), gy: 8 (over x, core).
Axes of the slice: x: 4, y: 4, z: 4, core: 2. Of those that a mesh axis runs over, the one named last changes fastest.
Arguments:
- states: float32 [8, 64, 64, 1024], P(None, None, 'gx', 'gy'), may hold values from -6 to 6
- swept_volume: float32 [4, 64, 1024], P(None, 'gx', 'gy'), may hold values from -3 to 3
- flux_own: float32 [4, 64, 64], replicated, may hold values from -0.75 to 0.75
- flux_next: float32 [4, 64, 64], replicated, may hold values from -0.75 to 0.75
- mass_inverse: float32 [64, 64], replicated, may hold values from -0.75 to 0.75
- projection: float32 [4, 64, 64], replicated, may hold values from -0.75 to 0.75
- new_owner: int32 [16, 8, 512, 4], P('gx', 'gy'), may hold values from 0 to 127, all different within a row; in each aligned block of 512 rows (0 to 511, 512 to 1023, ..., all dimensions but the last counted through in order) at most 32 rows name the same one
- new_slot: int32 [16, 8, 512, 4], P('gx', 'gy'), may hold values from 0 to 511
- intersection_weight: float32 [16, 8, 512, 4], P('gx', 'gy'), may hold values from 0.2 to 1
Outputs:
- remapped: float32 [8, 64, 65536], P(None, None, ('gx', 'gy'))
The draws below stay inside these ranges and needn't reach their ends.
Inputs may be any that keep to these rules, and one draw needn't show every extreme that they name: `new_owner`: each old element names 4 different owners; among the 512 old elements of one device no owner is named more than 32 times, a bound that some block reaches.
All inputs are finite; a program needn't handle non-finite values.
Results may differ from the reference program's by a relative error of at most 0.0003.
Values sent between devices are 32-bit elements; how exact they have to be, the bound alone decides.
A program may use at most 128 MiB of HBM per device.

```python
import math
import jax
import jax.numpy as jnp
import numpy as np
from jax import lax

F = 8
Q = 64
K = 4
EX = 4
EY = 128
CAP = 32
NXE = 64
NYE = 1024
N_GX = 16
N_GY = 8


def place_ends(values, key, smallest, top_value):
    spot = [jax.random.randint(jax.random.fold_in(key, axis), (), 0, length) for axis, length in enumerate(values.shape)]
    main_axis = values.shape.index(max(values.shape))
    beside = spot[:main_axis] + [(spot[main_axis] + 1) % values.shape[main_axis]] + spot[main_axis + 1:]
    return values.at[tuple(spot)].set(smallest).at[tuple(beside)].set(top_value)


def level_of(stream_key, extent, split, smallest, high):
    def one(dim, shards_of):
        heights = jax.random.uniform(jax.random.fold_in(jax.random.fold_in(stream_key, 6), dim), (shards_of,), jnp.float32, smallest / len(split), high / len(split))
        return jnp.repeat(jnp.exp(heights), extent[dim] // shards_of).reshape((-1,) + (1,) * (len(extent) - dim - 1))

    gain = one(*split[0])
    for cut in split[1:]:
        gain = gain * one(*cut)
    return gain


def routed_block(stream_key, own, number, rows, count, top, limit, lean):
    sequence = jax.random.permutation(stream_key, count)
    crowded, ordinary = load_shares(count, rows * top, limit, lean, True), load_shares(count, rows * top, limit, lean, False)
    places = jnp.arange(count)

    def named(sizes, offset_by):
        used = int((sizes > 0).sum())
        fixed = max(1, used // 4)
        shifted = fixed + (places - fixed + offset_by * (used - fixed)) % max(1, count - fixed)
        return jnp.zeros((count,), jnp.int32).at[sequence[jnp.where(places < fixed, places, shifted)]].set(jnp.asarray(sizes, jnp.int32))

    sizes = jnp.where(number % 4 == 0, named(crowded, number // 4), named(ordinary, number - number // 4 - 1))
    mixed = jax.random.permutation(jax.random.fold_in(own, 3), count)
    donor, sink = mixed[0:count // 2 * 2:2], mixed[1:count // 2 * 2:2]
    room = jnp.minimum(sizes[donor] - 1, limit - sizes[sink]) // 2
    room = jnp.where((donor == sequence[0]) | (sink == sequence[0]) | (sizes[sink] == 0), 0, jnp.maximum(room, 0))
    shifted = jax.random.randint(jax.random.fold_in(own, 4), (count // 2,), 0, 1 << 20) % (room + 1)
    sizes = sizes.at[donor].add(-shifted).at[sink].add(shifted)
    items = jnp.searchsorted(jnp.cumsum(sizes), jnp.arange(rows * top), side="right").astype(jnp.int32)
    listing = items.reshape(top, rows).T
    listing = listing[jax.random.permutation(jax.random.fold_in(own, 1), rows)]
    offset_by = jax.random.randint(jax.random.fold_in(own, 2), (rows, 1), 0, top)
    return jnp.take_along_axis(listing, (jnp.arange(top)[None, :] + offset_by) % top, axis=1)


def load_shares(amount, total, reach, slope, full):
    portions = [(1 << 20) // math.isqrt(standing ** slope) + 1 for standing in range(1, amount + 1)]
    largest = reach if full else min(reach, max(-(-total // amount), total * portions[0] // sum(portions)))
    least = 1 if total - largest >= amount - 1 else 0
    given, rest = [largest] + [least] * (amount - 1), total - largest - least * (amount - 1)
    while rest > 0:
        free = [i for i in range(1, amount) if given[i] < largest] or [i for i in range(1, amount) if given[i] < reach]
        pool, left = sum([portions[i] for i in free]), rest
        for i in free:
            extra = min(reach - given[i], max(1, left * portions[i] // pool), rest)
            given[i] = given[i] + extra
            rest = rest - extra
    return np.array(given)


def noise(own_key, extent, width, reach, pieces=(), dtype=jnp.bfloat16):
    factor_of = level_of(own_key, extent, pieces, -0.22, 0.18) if pieces else 1.0
    array = jax.random.normal(own_key, extent, jnp.float32) * width * factor_of
    return jnp.minimum(jnp.maximum(array, -reach), reach).astype(dtype)


def setup_inputs(seed: int = 0) -> dict:
    seeds = jax.random.split(jax.random.key(seed), 10)
    states = noise(seeds[0], (F, Q, NXE, NYE), 1.0, 6.0, ((2, 16), (3, 8)), jnp.float32)
    swept_volume = noise(seeds[1], (4, NXE, NYE), 0.5, 3.0, ((1, 16), (2, 8)), jnp.float32)
    flux_own = noise(seeds[2], (4, Q, Q), Q ** -0.5, 0.75, (), jnp.float32)
    flux_next = noise(seeds[3], (4, Q, Q), Q ** -0.5, 0.75, (), jnp.float32)
    mass_inverse = noise(seeds[4], (Q, Q), Q ** -0.5, 0.75, (), jnp.float32)
    projection = noise(seeds[5], (K, Q, Q), Q ** -0.5, 0.75, (), jnp.float32)
    new_owner_keys = jax.random.split(jax.random.fold_in(seeds[6], 1), N_GX * N_GY * (EX * EY) // (EX * EY))
    new_owner_turns = jax.random.permutation(jax.random.fold_in(seeds[6], 3), N_GX * N_GY * (EX * EY) // (EX * EY))
    new_owner = jax.vmap(lambda own, number: routed_block(jax.random.fold_in(seeds[6], 2), own, number, EX * EY, N_GX * N_GY, K, CAP, 2))(new_owner_keys, new_owner_turns).reshape((N_GX, N_GY, EX * EY, K))
    new_slot = place_ends(jax.random.randint(seeds[7], (N_GX, N_GY, EX * EY, K), 0, EX * EY), jax.random.fold_in(seeds[7], 1), 0, (EX * EY) - 1).astype(jnp.int32)
    intersection_weight = jnp.clip(jnp.exp(math.log(1.0) - 1.609438 * jax.random.uniform(seeds[8], (N_GX, N_GY, EX * EY, K), jnp.float32) ** level_of(seeds[8], (N_GX, N_GY, EX * EY, K), ((0, 16), (1, 8)), -0.2, 0.2)), 0.2, 1.0)
    return dict(states=states, swept_volume=swept_volume, flux_own=flux_own, flux_next=flux_next, mass_inverse=mass_inverse, projection=projection, new_owner=new_owner, new_slot=new_slot, intersection_weight=intersection_weight)


PRECISE = lax.Precision.HIGHEST
MARGIN = 0.75


def nodal_product(matrix, values):
    return jnp.einsum("pq,fqxy->fpxy", matrix, values, precision=PRECISE)


def advance(padded, volumes, flux_own, flux_next, mass_inverse):
    center = padded[:, :, 1:-1, 1:-1]
    beside = (padded[:, :, :-2, 1:-1], padded[:, :, 2:, 1:-1], padded[:, :, 1:-1, :-2], padded[:, :, 1:-1, 2:])
    summed = jnp.zeros(center.shape, jnp.float32)
    for side_index in range(4):
        outward = jnp.maximum(volumes[side_index], 0.0)
        inward = jnp.minimum(volumes[side_index], 0.0)
        summed = summed + outward * nodal_product(flux_own[side_index], center) + inward * nodal_product(flux_next[side_index], beside[side_index])
    return center - nodal_product(mass_inverse, summed)


def limit_nodes(advanced, padded_means):
    center = padded_means[:, 1:-1, 1:-1]
    neighbours = (padded_means[:, :-2, 1:-1], padded_means[:, 2:, 1:-1], padded_means[:, 1:-1, :-2], padded_means[:, 1:-1, 2:])
    lower_bound = center
    upper_bound = center
    for neighbour in neighbours:
        lower_bound = jnp.minimum(lower_bound, neighbour)
        upper_bound = jnp.maximum(upper_bound, neighbour)
    return jnp.clip(advanced, (lower_bound - MARGIN)[:, None], (upper_bound + MARGIN)[:, None])


def element_grid(values):
    slots_each = values.shape[-1]
    shaped = values.reshape(N_GX, N_GY, EX, EY, slots_each)
    return jnp.transpose(shaped, (4, 0, 2, 1, 3)).reshape(slots_each, N_GX * EX, N_GY * EY)


def reference(states, swept_volume, flux_own, flux_next, mass_inverse, projection, new_owner, new_slot, intersection_weight):
    owners = element_grid(new_owner)
    slots = element_grid(new_slot)
    weights = element_grid(intersection_weight)
    target = (owners * (EX * EY) + slots).reshape(-1).astype(jnp.int32)
    total_new = N_GX * N_GY * EX * EY

    def one_field(field_values):
        single = field_values[None]
        padded = jnp.pad(single, ((0, 0), (0, 0), (1, 1), (1, 1)))
        advanced = advance(padded, swept_volume, flux_own, flux_next, mass_inverse)
        cell_means = jnp.mean(advanced, axis=1)
        padded_means = jnp.pad(cell_means, ((0, 0), (1, 1), (1, 1)), mode="edge")
        limited = limit_nodes(advanced, padded_means)[0]
        projected = jnp.einsum("kpq,qxy->kpxy", projection, limited, precision=PRECISE) * weights[:, None]
        columns = jnp.transpose(projected, (1, 0, 2, 3)).reshape(limited.shape[0], -1)
        summed = jnp.zeros((limited.shape[0], total_new), jnp.float32).at[:, target].add(columns)
        return jnp.dot(mass_inverse, summed, precision=PRECISE, preferred_element_type=jnp.float32)

    return lax.map(one_field, states)
```

```python
import functools

import jax
import jax.numpy as jnp
from jax import lax
from jax.experimental import pallas as pl
from jax.experimental.pallas import tpu as pltpu
from jax.sharding import PartitionSpec as P

F, Q, K, EX, EY, CAP = 8, 64, 4, 4, 128, 32
E = EX * EY
COLS = F * Q
MARGIN = 0.75
MESH = pl.DeviceIdType.MESH
VMEM = pl.BlockSpec(memory_space=pltpu.VMEM)
F32, BF16 = jnp.float32, jnp.bfloat16
PARTS = ((0, 3, "xyz"), (3, 3, "yzx"), (6, 2, "zxy"))


def halves(values):
    high = values.astype(BF16)
    return high, (values - high.astype(F32)).astype(BF16)


def product(matrix, values):
    high, low = halves(values)
    stacked = jnp.concatenate([high, low, high], axis=0)
    return jnp.dot(matrix, stacked, preferred_element_type=F32)


def tables_kernel(rows_ref, inverse_ref, flux_ref, project_ref, table_ref, g_ref, p_ref):
    inverse = inverse_ref[...]
    for source, target, count in ((flux_ref, g_ref, 8), (project_ref, p_ref, 4)):
        for term in range(count):
            made = jnp.dot(
                inverse,
                source[term],
                precision=lax.Precision.HIGHEST,
                preferred_element_type=F32,
            )
            high, low = halves(made)
            target[term * Q : (term + 1) * Q, :] = jnp.concatenate([high, high, low], axis=1)
    devices = lax.broadcasted_iota(jnp.int32, (128, 256), 0).astype(F32)
    ranks = lax.broadcasted_iota(jnp.int32, (CAP, 256), 0).astype(F32)
    earlier = (
        lax.broadcasted_iota(jnp.int32, (256, 256), 0)
        < lax.broadcasted_iota(jnp.int32, (256, 256), 1)
    )
    earlier = jnp.where(earlier, 1.0, 0.0).astype(BF16)
    carry = jnp.zeros((128, 1), F32)
    table = jnp.zeros((128, 8 * CAP), F32)
    for chunk in range(E * K // 256):
        lanes = slice(chunk * 256, (chunk + 1) * 256)
        named = jnp.where(devices == rows_ref[0:1, lanes], 1.0, 0.0)
        before = jnp.dot(named.astype(BF16), earlier, preferred_element_type=F32) + carry
        rank = jnp.sum(named * before, axis=0, keepdims=True)
        carry = carry + jnp.sum(named, axis=1, keepdims=True)
        placed = ranks == rank
        weight = rows_ref[6:7, lanes]
        first = weight.astype(BF16).astype(F32)
        second = (weight - first).astype(BF16).astype(F32)
        parts = [rows_ref[1 + m : 2 + m, lanes] for m in range(5)]
        parts += [first, second, weight - first - second]
        values = jnp.concatenate([jnp.where(placed, row, 0.0) for row in parts], axis=0)
        table = table + lax.dot_general(
            named.astype(BF16),
            values.astype(BF16),
            (((1,), (1,)), ((), ())),
            preferred_element_type=F32,
        )
    table_ref[...] = table


def make_tables(new_owner, new_slot, weight, mass_inverse, flux, projection):
    owner = new_owner.reshape(E, K).T.reshape(E * K)
    slot = new_slot.reshape(E, K).T.reshape(E * K)
    weight = weight.reshape(E, K).T.reshape(E * K)
    which = jnp.arange(E * K, dtype=jnp.int32)
    element = which % E + 1
    rows = jnp.stack(
        [
            owner.astype(F32),
            (element // 128).astype(F32),
            (element % 128).astype(F32),
            (which // E).astype(F32),
            (slot // 128).astype(F32),
            (slot % 128).astype(F32),
            weight,
        ]
        + [jnp.zeros((E * K,), F32)]
    )
    table, g, p = pl.pallas_call(
        tables_kernel,
        out_shape=(
            jax.ShapeDtypeStruct((128, 8 * CAP), F32),
            jax.ShapeDtypeStruct((8 * Q, 3 * Q), BF16),
            jax.ShapeDtypeStruct((4 * Q, 3 * Q), BF16),
        ),
        in_specs=[VMEM] * 4,
        out_specs=[VMEM] * 3,
    )(rows, mass_inverse, flux, projection)
    t = table.reshape(4, 4, 4, 2, 8, CAP)
    full = jnp.stack(
        [
            t[..., 0, :] * 128 + t[..., 1, :] - 1,
            t[..., 2, :],
            t[..., 3, :] * 128 + t[..., 4, :],
            t[..., 5, :] + t[..., 6, :] + t[..., 7, :],
        ],
        axis=4,
    )
    full = jnp.pad(full, [(0, 0)] * 4 + [(0, 4), (0, 0)])
    spot = {"z": 0, "y": 1, "x": 2}
    made = []
    for _, _, (a, b, c) in PARTS:
        order = (spot[a], spot[b], 3, 4, spot[c], 5)
        made.append(jnp.transpose(full, order).reshape(4, 8, 8, 128))
    return made, g, p


def flux_kernel(
    u_ref, v_ref, g_ref, out_ref, sides, packed, means, mean_sides, mean_packed, bounds, send, recv
):
    gx, gy = lax.axis_index("gx"), lax.axis_index("gy")
    n_x, n_y = lax.axis_size("gx"), lax.axis_size("gy")
    near = (
        (lax.rem(gx + n_x - 1, n_x), gy),
        (lax.rem(gx + 1, n_x), gy),
        (gx, lax.rem(gy + n_y - 1, n_y)),
        (gx, lax.rem(gy + 1, n_y)),
    )
    inside = (gx > 0, gx < n_x - 1, gy > 0, gy < n_y - 1)
    barrier = pltpu.get_barrier_semaphore()
    for device in near:
        pl.semaphore_signal(barrier, inc=1, device_id=device, device_id_type=MESH)
    lane64 = lax.broadcasted_iota(jnp.int32, (Q, EY), 1)
    lane8 = lax.broadcasted_iota(jnp.int32, (8, EY), 1)
    field8 = lax.broadcasted_iota(jnp.int32, (8, EY), 0)

    def block(j):
        return slice(j * EY, (j + 1) * EY)

    def pack(f, _):
        rows = pl.ds(pl.multiple_of(f * Q, Q), Q)
        low = jnp.zeros((Q, EY), F32)
        high = jnp.zeros((Q, EY), F32)
        for j in range(EX):
            values = u_ref[rows, block(j)]
            low = jnp.where(lane64 == j, pltpu.roll(values, j, 1), low)
            high = jnp.where(lane64 == j, pltpu.roll(values, j + 1, 1), high)
        packed[0, rows, :] = low
        packed[1, rows, :] = high
        return 0

    lax.fori_loop(0, F, pack, 0)
    pl.semaphore_wait(barrier, 4)

    def exchange(sources, target, base):
        copies = []
        for s in range(4):
            copies.append(
                pltpu.make_async_remote_copy(
                    src_ref=sources[s],
                    dst_ref=target.at[s ^ 1],
                    send_sem=send.at[base + s],
                    recv_sem=recv.at[base + (s ^ 1)],
                    device_id=near[s],
                    device_id_type=MESH,
                )
            )
        for copy in copies:
            copy.start()
        return copies

    copies = exchange(
        (
            u_ref.at[:, pl.ds(0, EY)],
            u_ref.at[:, pl.ds(3 * EY, EY)],
            packed.at[0],
            packed.at[1],
        ),
        sides,
        0,
    )

    def interior(f, _):
        rows = pl.ds(pl.multiple_of(f * Q, Q), Q)
        u = u_ref[rows, :]
        made = product(g_ref[...], u)
        for j in range(EX):
            total = u[:, block(j)]
            for s in range(4):
                outward = jnp.maximum(v_ref[s : s + 1, block(j)], 0.0)
                total = total - outward * made[s * Q : (s + 1) * Q, block(j)]
            inward = [jnp.minimum(v_ref[s : s + 1, block(j)], 0.0) for s in range(4)]
            if j > 0:
                total = total - inward[0] * made[4 * Q : 5 * Q, block(j - 1)]
            if j < EX - 1:
                total = total - inward[1] * made[5 * Q : 6 * Q, block(j + 1)]
            before = pltpu.roll(made[6 * Q : 7 * Q, block(j)], 1, 1)
            after = pltpu.roll(made[7 * Q : 8 * Q, block(j)], EY - 1, 1)
            total = total - jnp.where(lane64 == 0, 0.0, inward[2] * before)
            total = total - jnp.where(lane64 == EY - 1, 0.0, inward[3] * after)
            out_ref[rows, block(j)] = total
        return 0

    lax.fori_loop(0, F, interior, 0)
    for copy in copies:
        copy.wait()
    gate = [jnp.where(here, 1.0, 0.0).astype(F32) for here in inside]

    def edges(f, found):
        found = list(found)
        rows = pl.ds(pl.multiple_of(f * Q, Q), Q)
        made = [
            product(g_ref[(4 + s) * Q : (5 + s) * Q, :], sides[s, rows, :]) for s in range(4)
        ]
        for j in range(EX):
            inward = [jnp.minimum(v_ref[s : s + 1, block(j)], 0.0) * gate[s] for s in range(4)]
            total = out_ref[rows, block(j)]
            if j == 0:
                total = total - inward[0] * made[0]
            if j == EX - 1:
                total = total - inward[1] * made[1]
            before = made[2] if j == 0 else pltpu.roll(made[2], EY - j, 1)
            after = pltpu.roll(made[3], EY - 1 - j, 1)
            total = total - jnp.where(lane64 == 0, inward[2] * before, 0.0)
            total = total - jnp.where(lane64 == EY - 1, inward[3] * after, 0.0)
            out_ref[rows, block(j)] = total
            mean = jnp.sum(total, axis=0, keepdims=True) * (1.0 / Q)
            found[j] = jnp.where(field8 == f, mean, found[j])
        return tuple(found)

    found = lax.fori_loop(0, F, edges, tuple(jnp.zeros((8, EY), F32) for _ in range(EX)))
    for j in range(EX):
        means[:, block(j)] = found[j]
    low = jnp.zeros((8, EY), F32)
    high = jnp.zeros((8, EY), F32)
    for j in range(EX):
        values = means[:, block(j)]
        low = jnp.where(lane8 == j, pltpu.roll(values, j, 1), low)
        high = jnp.where(lane8 == j, pltpu.roll(values, j + 1, 1), high)
    mean_packed[0] = low
    mean_packed[1] = high
    copies = exchange(
        (
            means.at[:, pl.ds(0, EY)],
            means.at[:, pl.ds(3 * EY, EY)],
            mean_packed.at[0],
            mean_packed.at[1],
        ),
        mean_sides,
        4,
    )
    for copy in copies:
        copy.wait()
    for j in range(EX):
        center = means[:, block(j)]
        left = means[:, block(j - 1)] if j > 0 else jnp.where(gate[0] > 0, mean_sides[0], center)
        right = (
            means[:, block(j + 1)] if j < EX - 1 else jnp.where(gate[1] > 0, mean_sides[1], center)
        )
        before = mean_sides[2] if j == 0 else pltpu.roll(mean_sides[2], EY - j, 1)
        before = jnp.where(gate[2] > 0, before, center)
        before = jnp.where(lane8 == 0, before, pltpu.roll(center, 1, 1))
        after = pltpu.roll(mean_sides[3], EY - 1 - j, 1)
        after = jnp.where(gate[3] > 0, after, center)
        after = jnp.where(lane8 == EY - 1, after, pltpu.roll(center, EY - 1, 1))
        lower, upper = center, center
        for other in (left, right, before, after):
            lower = jnp.minimum(lower, other)
            upper = jnp.maximum(upper, other)
        bounds[0, :, block(j)] = lower - MARGIN
        bounds[1, :, block(j)] = upper + MARGIN

    for f in range(F):
        rows = slice(f * Q, (f + 1) * Q)
        lower = bounds[0, f : f + 1, :]
        upper = bounds[1, f : f + 1, :]
        out_ref[rows, :] = jnp.minimum(jnp.maximum(out_ref[rows, :], lower), upper)


def advance_and_limit(states, volumes, g):
    return pl.pallas_call(
        flux_kernel,
        out_shape=jax.ShapeDtypeStruct((COLS, E), F32),
        in_specs=[VMEM] * 3,
        out_specs=VMEM,
        scratch_shapes=[
            pltpu.VMEM((4, COLS, EY), F32),
            pltpu.VMEM((2, COLS, EY), F32),
            pltpu.VMEM((8, E), F32),
            pltpu.VMEM((4, 8, EY), F32),
            pltpu.VMEM((2, 8, EY), F32),
            pltpu.VMEM((2, 8, E), F32),
            pltpu.SemaphoreType.DMA((8,)),
            pltpu.SemaphoreType.DMA((8,)),
        ],
        compiler_params=pltpu.CompilerParams(
            collective_id=0, has_side_effects=True, vmem_limit_bytes=24 * 2**20
        ),
    )(states, volumes, g)


def remap_kernel(
    lim_ref, t0, t1, t2, p_ref, out_ref,
    ar0, ar1, ar2, at0, at1, at2, bs0, bs1, bs2, br0, br1, br2,
    cs0, cs1, cs2, cr0, cr1, cr2, split, picked, pair,
    a_send, a_recv, t_send, t_recv, b_send, b_recv, c_send, c_recv, own_sem,
):
    tables, ar, at = (t0, t1, t2), (ar0, ar1, ar2), (at0, at1, at2)
    bs, br, cs, cr = (bs0, bs1, bs2), (br0, br1, br2), (cs0, cs1, cs2), (cr0, cr1, cr2)
    gx, gy = lax.axis_index("gx"), lax.axis_index("gy")
    here = {"x": gy // 2, "y": lax.rem(gx, 4), "z": gx // 4, "c": lax.rem(gy, 2)}

    def away(axis, distance, core=0):
        at_ = dict(here)
        at_[axis] = lax.rem(here[axis] + distance, 4)
        at_["c"] = lax.rem(here["c"] + core, 2)
        return (at_["z"] * 4 + at_["y"], at_["x"] * 2 + at_["c"])

    barrier = pltpu.get_barrier_semaphore()
    for axis in "xyz":
        for distance in (1, 2, 3):
            for core in (0, 1):
                pl.semaphore_signal(
                    barrier, inc=1, device_id=away(axis, distance, core), device_id_type=MESH
                )
    pl.semaphore_signal(barrier, inc=1, device_id=away("x", 0, 1), device_id_type=MESH)
    pl.semaphore_wait(barrier, 19)

    def states_copy(p, d):
        first, count, axes = PARTS[p]
        return pltpu.make_async_remote_copy(
            src_ref=lim_ref.at[pl.ds(first * Q, count * Q)],
            dst_ref=ar[p].at[3 - d],
            send_sem=a_send.at[p, d - 1],
            recv_sem=a_recv.at[p, d - 1],
            device_id=away(axes[0], d),
            device_id_type=MESH,
        )

    def table_copy(p, d):
        axis = PARTS[p][2][0]
        return pltpu.make_async_remote_copy(
            src_ref=tables[p].at[lax.rem(here[axis] + d, 4)],
            dst_ref=at[p].at[4 - d],
            send_sem=t_send.at[p, d - 1],
            recv_sem=t_recv.at[p, d - 1],
            device_id=away(axis, d),
            device_id_type=MESH,
        )

    def block_copy(p, d, core):
        axis = PARTS[p][2][1]
        return pltpu.make_async_remote_copy(
            src_ref=bs[p].at[d, lax.rem(here["c"] + core, 2)],
            dst_ref=br[p].at[lax.rem(4 - d, 4), :, :, pl.ds(core * 128, 128)],
            send_sem=b_send.at[p, d, core],
            recv_sem=b_recv.at[p, d, core],
            device_id=away(axis, d, core),
            device_id_type=MESH,
        )

    def own_copy(p):
        return pltpu.make_async_copy(
            bs[p].at[0, here["c"]], br[p].at[0, :, :, pl.ds(0, 128)], own_sem.at[p]
        )

    def sum_copy(p, d):
        axis = PARTS[p][2][2]
        return pltpu.make_async_remote_copy(
            src_ref=cs[p].at[lax.rem(here[axis] + d, 4)],
            dst_ref=cr[p].at[d - 1],
            send_sem=c_send.at[p, d - 1],
            recv_sem=c_recv.at[p, d - 1],
            device_id=away(axis, d),
            device_id_type=MESH,
        )

    for d in (2, 1, 3):
        for p in range(3):
            table_copy(p, d).start()
    for d in (2, 1, 3):
        for p in range(3):
            states_copy(p, d).start()

    element = lax.broadcasted_iota(jnp.int32, (E, 256), 0).astype(F32)
    quarter = lax.rem(lax.broadcasted_iota(jnp.int32, (1, 256), 1) // CAP, 4)

    def route(p):
        first, count, axes = PARTS[p]
        rows = count * Q
        me_a, me_b = here[axes[0]], here[axes[1]]
        at[p][0] = tables[p][me_a]
        for d in (0, 1, 3, 2):
            if d:
                states_copy(p, d).wait_recv()
                table_copy(p, d).wait_recv()
            j = (4 - d) % 4
            values = lim_ref[first * Q : first * Q + rows, :] if d == 0 else ar[p][3 - d]
            high, low = halves(values)
            split[j, 0:rows, :] = high
            split[j, rows : 2 * rows, :] = low

        def towards(step, _):
            d = 3 - step
            group = lax.rem(me_b + d, 4) * 2
            infos = []
            for j in range(4):
                info = jnp.concatenate(
                    [pltpu.roll(at[p][j, group + c], CAP * j, 1) if j else at[p][j, group + c] for c in range(2)],
                    axis=1,
                )
                infos.append(info)
                hot = jnp.where(element == info[0:1, :], 1.0, 0.0).astype(BF16)
                made = jnp.dot(split[j, 0 : 2 * rows, :], hot, preferred_element_type=F32)
                picked[j, 0:rows, :] = made[0:rows] + made[rows:]
            for o in range(4):
                info = infos[3]
                for j in range(3):
                    info = jnp.where(quarter == (o + j) % 4, infos[j], info)
                which, weight = info[1:2, :], info[3:4, :]
                for f in range(count):
                    part = slice(f * Q, (f + 1) * Q)
                    values = picked[3, part, :]
                    for j in range(3):
                        values = jnp.where(quarter == (o + j) % 4, picked[j, part, :], values)
                    made = product(p_ref[...], values)
                    chosen = made[3 * Q :]
                    for k in range(3):
                        chosen = jnp.where(which == float(k), made[k * Q : (k + 1) * Q], chosen)
                    chosen = chosen * weight
                    bs[p][d, 0, o, part, :] = chosen[:, 0:128]
                    bs[p][d, 1, o, part, :] = chosen[:, 128:256]
                bs[p][d, 0, o, rows : rows + 8, :] = info[:, 0:128]
                bs[p][d, 1, o, rows : rows + 8, :] = info[:, 128:256]
            block_copy(p, d, 1).start()

            @pl.when(d > 0)
            def _():
                block_copy(p, d, 0).start()

            return 0

        lax.fori_loop(0, 4, towards, 0)
        own_copy(p).start()

    def gather(p):
        _, count, axes = PARTS[p]
        rows = count * Q
        me_c = here[axes[2]]
        for number, d in enumerate((0, 1, 3, 2)):
            if d == 0:
                own_copy(p).wait()
                block_copy(p, 0, 1).wait_recv()
            else:
                block_copy(p, d, 0).wait_recv()
                block_copy(p, d, 1).wait_recv()
            slot_of = (4 - d) % 4

            def owner(step, _, number=number, slot_of=slot_of):
                distance = lax.rem(step + 2, 4)
                o = lax.rem(me_c + distance, 4)
                high, low = halves(br[p][slot_of, o, 0:rows, :])
                pair[0:rows, :] = high
                pair[rows : 2 * rows, :] = low
                hot = jnp.where(element == br[p][slot_of, o, rows + 2 : rows + 3, :], 1.0, 0.0)
                made = lax.dot_general(
                    pair[0 : 2 * rows, :],
                    hot.astype(BF16),
                    (((1,), (1,)), ((), ())),
                    preferred_element_type=F32,
                )
                total = made[0:rows] + made[rows:]
                if number > 0:
                    total = total + cs[p][o]
                cs[p][o] = total
                if number == 3:

                    @pl.when(distance > 0)
                    def _():
                        sum_copy(p, distance).start()

                return 0

            lax.fori_loop(0, 4, owner, 0)

    def finish(p):
        first, count, axes = PARTS[p]
        total = cs[p][here[axes[2]]]
        for d in (1, 3, 2):
            sum_copy(p, d).wait_recv()
            total = total + cr[p][d - 1]
        out_ref[first * Q : (first + count) * Q, :] = total

    for p in range(3):
        route(p)
    for p in (2, 0, 1):
        gather(p)
    for p in (2, 0, 1):
        finish(p)
    for p in range(3):
        for d in (1, 2, 3):
            states_copy(p, d).wait_send()
            table_copy(p, d).wait_send()
            block_copy(p, d, 0).wait_send()
            block_copy(p, d, 1).wait_send()
            sum_copy(p, d).wait_send()
        block_copy(p, 0, 1).wait_send()


def remap(limited, tables, p):
    rows = [count * Q for _, count, _ in PARTS]
    dma = pltpu.SemaphoreType.DMA
    return pl.pallas_call(
        remap_kernel,
        out_shape=jax.ShapeDtypeStruct((COLS, E), F32),
        in_specs=[VMEM] * 5,
        out_specs=VMEM,
        scratch_shapes=[pltpu.VMEM((3, r, E), F32) for r in rows]
        + [pltpu.VMEM((4, 8, 8, 128), F32) for r in rows]
        + [pltpu.VMEM((4, 2, 4, r + 8, 128), F32) for r in rows]
        + [pltpu.VMEM((4, 4, r + 8, 256), F32) for r in rows]
        + [pltpu.VMEM((4, r, E), F32) for r in rows]
        + [pltpu.VMEM((3, r, E), F32) for r in rows]
        + [
            pltpu.VMEM((4, 2 * max(rows), E), BF16),
            pltpu.VMEM((4, max(rows), 256), F32),
            pltpu.VMEM((2 * max(rows), 256), BF16),
            dma((3, 3)),
            dma((3, 3)),
            dma((3, 3)),
            dma((3, 3)),
            dma((3, 4, 2)),
            dma((3, 4, 2)),
            dma((3, 3)),
            dma((3, 3)),
            dma((3,)),
        ],
        compiler_params=pltpu.CompilerParams(
            collective_id=1, has_side_effects=True, vmem_limit_bytes=56 * 2**20
        ),
    )(limited, *tables, p)


def body(
    states,
    swept_volume,
    flux_own,
    flux_next,
    mass_inverse,
    projection,
    new_owner,
    new_slot,
    intersection_weight,
):
    flux = jnp.concatenate([flux_own, flux_next], axis=0)
    tables, g, p = make_tables(
        new_owner, new_slot, intersection_weight, mass_inverse, flux, projection
    )
    limited = advance_and_limit(states.reshape(COLS, E), swept_volume.reshape(4, E), g)
    return remap(limited, tables, p).reshape(F, Q, E)


def solution(mesh):
    placed = (
        P(None, None, "gx", "gy"),
        P(None, "gx", "gy"),
        P(),
        P(),
        P(),
        P(),
        P("gx", "gy", None, None),
        P("gx", "gy", None, None),
        P("gx", "gy", None, None),
    )
    return jax.shard_map(
        body, mesh=mesh, in_specs=placed, out_specs=P(None, None, ("gx", "gy")), check_vma=False
    )
```

```python
import functools

import jax
import jax.numpy as jnp
from jax import lax
from jax.experimental import pallas as pl
from jax.experimental.pallas import tpu as pltpu
from jax.sharding import PartitionSpec as P

F, Q, K, EX, EY, CAP = 8, 64, 4, 4, 128, 32
E = EX * EY
COLS = F * Q
MARGIN = 0.75
MESH = pl.DeviceIdType.MESH
VMEM = pl.BlockSpec(memory_space=pltpu.VMEM)
F32, BF16 = jnp.float32, jnp.bfloat16
PARTS = ((0, 3, "xyz"), (3, 3, "yzx"), (6, 2, "zxy"))


def halves(values):
    high = values.astype(BF16)
    return high, (values - high.astype(F32)).astype(BF16)


def product(matrix, values):
    high, low = halves(values)
    stacked = jnp.concatenate([high, low, high], axis=0)
    return jnp.dot(matrix, stacked, preferred_element_type=F32)


def fold(inverse_ref, sources, target_ref):
    inverse = inverse_ref[...]
    for term, source in enumerate(sources):
        made = jnp.dot(
            inverse, source, precision=lax.Precision.HIGHEST, preferred_element_type=F32
        )
        high, low = halves(made)
        target_ref[term * Q : (term + 1) * Q, :] = jnp.concatenate([high, high, low], axis=1)


def rank_table(rows_ref):
    devices = lax.broadcasted_iota(jnp.int32, (128, 256), 0).astype(F32)
    ranks = lax.broadcasted_iota(jnp.int32, (CAP, 256), 0).astype(F32)
    earlier = lax.broadcasted_iota(jnp.int32, (256, 256), 0) < lax.broadcasted_iota(
        jnp.int32, (256, 256), 1
    )
    earlier = jnp.where(earlier, 1.0, 0.0).astype(BF16)
    carry = jnp.zeros((128, 1), F32)
    table = jnp.zeros((128, 8 * CAP), F32)
    for chunk in range(E * K // 256):
        lanes = slice(chunk * 256, (chunk + 1) * 256)
        named = jnp.where(devices == rows_ref[0:1, lanes], 1.0, 0.0)
        before = jnp.dot(named.astype(BF16), earlier, preferred_element_type=F32) + carry
        rank = jnp.sum(named * before, axis=0, keepdims=True)
        carry = carry + jnp.sum(named, axis=1, keepdims=True)
        placed = ranks == rank
        weight = rows_ref[6:7, lanes]
        first = weight.astype(BF16).astype(F32)
        second = (weight - first).astype(BF16).astype(F32)
        parts = [rows_ref[1 + m : 2 + m, lanes] for m in range(5)]
        parts += [first, second, weight - first - second]
        values = jnp.concatenate([jnp.where(placed, row, 0.0) for row in parts], axis=0)
        table = table + lax.dot_general(
            named.astype(BF16),
            values.astype(BF16),
            (((1,), (1,)), ((), ())),
            preferred_element_type=F32,
        )
    return table.astype(BF16)


STRIDE = {"z": 32, "y": 8, "x": 2}


def part_table(table, axes, target_ref):
    a, b, c = axes
    row = lax.broadcasted_iota(jnp.int32, (32, 128), 0)
    lane = lax.broadcasted_iota(jnp.int32, (32, 128), 1)
    first = (row // 8) * STRIDE[a] + lax.rem(row // 2, 4) * STRIDE[b] + lax.rem(row, 2)
    quarter = lane // CAP
    made = [jnp.zeros((32, 128), F32)] * 8
    for o in range(4):
        chosen = jnp.where(lane == first + o * STRIDE[c], 1.0, 0.0).astype(BF16)
        found = jnp.dot(chosen, table, preferred_element_type=F32)
        for m in range(8):
            tile = found[:, (m // 4) * 128 : (m // 4 + 1) * 128]
            turn = (o - m % 4) % 4
            tile = pltpu.roll(tile, turn * CAP, 1) if turn else tile
            made[m] = jnp.where(quarter == o, tile, made[m])
    whats = (
        made[0] * 128 + made[1] - 1,
        made[2],
        made[3] * 128 + made[4],
        made[5] + made[6] + made[7],
    )
    for place in range(4):
        for number, what in enumerate(whats):
            target_ref[place, number] = what[place * 8 : (place + 1) * 8]


def kernel(
    u_ref, v_ref, inverse_ref, own_ref, next_ref, project_ref, rows_ref, out_ref,
    g_ref, p_ref, lim_ref, sides, packed, means, mean_sides, mean_packed,
    tb0, tb1, tb2, ar0, ar1, ar2, at0, at1, at2, bs0, bs1, bs2, br0, br1, br2,
    cs0, cs1, cs2, cr0, cr1, cr2, split, picked, pair,
    h_send, h_recv, m_send, m_recv,
    a_send, a_recv, t_send, t_recv, b_send, b_recv, c_send, c_recv, own_sem,
):
    tables, ar, at = (tb0, tb1, tb2), (ar0, ar1, ar2), (at0, at1, at2)
    bs, br, cs, cr = (bs0, bs1, bs2), (br0, br1, br2), (cs0, cs1, cs2), (cr0, cr1, cr2)
    gx, gy = lax.axis_index("gx"), lax.axis_index("gy")
    n_x, n_y = lax.axis_size("gx"), lax.axis_size("gy")
    here = {"x": gy // 2, "y": lax.rem(gx, 4), "z": gx // 4, "c": lax.rem(gy, 2)}
    near = (
        (lax.rem(gx + n_x - 1, n_x), gy),
        (lax.rem(gx + 1, n_x), gy),
        (gx, lax.rem(gy + n_y - 1, n_y)),
        (gx, lax.rem(gy + 1, n_y)),
    )
    inside = (gx > 0, gx < n_x - 1, gy > 0, gy < n_y - 1)
    gate = [jnp.where(there, 1.0, 0.0).astype(F32) for there in inside]

    def away(axis, distance, core=0):
        at_ = dict(here)
        at_[axis] = lax.rem(here[axis] + distance, 4)
        at_["c"] = lax.rem(here["c"] + core, 2)
        return (at_["z"] * 4 + at_["y"], at_["x"] * 2 + at_["c"])

    partners = [away(axis, d, core) for axis in "xyz" for d in (1, 2, 3) for core in (0, 1)]
    partners += [away("x", 0, 1), *near]
    barrier = pltpu.get_barrier_semaphore()
    for device in partners:
        pl.semaphore_signal(barrier, inc=1, device_id=device, device_id_type=MESH)

    def remote(source, target, send, recv, device):
        return pltpu.make_async_remote_copy(
            src_ref=source,
            dst_ref=target,
            send_sem=send,
            recv_sem=recv,
            device_id=device,
            device_id_type=MESH,
        )

    def rows_of(p):
        first, count, _ = PARTS[p]
        return pl.ds(first * Q, count * Q)

    def side_copy(p, s):
        rows = rows_of(p)
        source = (
            u_ref.at[rows, pl.ds(0, EY)],
            u_ref.at[rows, pl.ds(3 * EY, EY)],
            packed.at[0, rows],
            packed.at[1, rows],
        )[s]
        return remote(
            source, sides.at[s ^ 1, rows], h_send.at[p, s], h_recv.at[p, s ^ 1], near[s]
        )

    def mean_copy(p, s):
        source = (
            means.at[p, :, pl.ds(0, EY)],
            means.at[p, :, pl.ds(3 * EY, EY)],
            mean_packed.at[p, 0],
            mean_packed.at[p, 1],
        )[s]
        return remote(
            source, mean_sides.at[p, s ^ 1], m_send.at[p, s], m_recv.at[p, s ^ 1], near[s]
        )

    def states_copy(p, d):
        return remote(
            lim_ref.at[rows_of(p)],
            ar[p].at[3 - d],
            a_send.at[p, d - 1],
            a_recv.at[p, d - 1],
            away(PARTS[p][2][0], d),
        )

    def table_copy(p, d):
        axis = PARTS[p][2][0]
        return remote(
            tables[p].at[lax.rem(here[axis] + d, 4)],
            at[p].at[4 - d],
            t_send.at[p, d - 1],
            t_recv.at[p, d - 1],
            away(axis, d),
        )

    def block_copy(p, d, core):
        return remote(
            bs[p].at[d, lax.rem(here["c"] + core, 2)],
            br[p].at[lax.rem(4 - d, 4), :, :, pl.ds(core * 128, 128)],
            b_send.at[p, d, core],
            b_recv.at[p, d, core],
            away(PARTS[p][2][1], d, core),
        )

    def own_copy(p):
        return pltpu.make_async_copy(
            bs[p].at[0, here["c"]], br[p].at[0, :, :, pl.ds(0, 128)], own_sem.at[p]
        )

    def sum_copy(p, d):
        axis = PARTS[p][2][2]
        return remote(
            cs[p].at[lax.rem(here[axis] + d, 4)],
            cr[p].at[d - 1],
            c_send.at[p, d - 1],
            c_recv.at[p, d - 1],
            away(axis, d),
        )

    lane64 = lax.broadcasted_iota(jnp.int32, (Q, EY), 1)
    lane8 = lax.broadcasted_iota(jnp.int32, (8, EY), 1)
    row8 = lax.broadcasted_iota(jnp.int32, (8, EY), 0)

    def block(j):
        return slice(j * EY, (j + 1) * EY)

    def pack(f, _):
        rows = pl.ds(pl.multiple_of(f * Q, Q), Q)
        low = jnp.zeros((Q, EY), F32)
        high = jnp.zeros((Q, EY), F32)
        for j in range(EX):
            values = u_ref[rows, block(j)]
            low = jnp.where(lane64 == j, pltpu.roll(values, j, 1) if j else values, low)
            high = jnp.where(lane64 == j, pltpu.roll(values, j + 1, 1), high)
        packed[0, rows, :] = low
        packed[1, rows, :] = high
        return 0

    lax.fori_loop(0, F, pack, 0)
    pl.semaphore_wait(barrier, len(partners))
    for p in range(3):
        for s in range(4):
            side_copy(p, s).start()
    fold(inverse_ref, [own_ref[s] for s in range(4)] + [next_ref[s] for s in range(4)], g_ref)
    fold(inverse_ref, [project_ref[k] for k in range(4)], p_ref)

    def interior(f, _):
        rows = pl.ds(pl.multiple_of(f * Q, Q), Q)
        u = u_ref[rows, :]
        made = product(g_ref[...], u)
        for j in range(EX):
            total = u[:, block(j)]
            for s in range(4):
                outward = jnp.maximum(v_ref[s, j : j + 1, :], 0.0)
                total = total - outward * made[s * Q : (s + 1) * Q, block(j)]
            inward = [jnp.minimum(v_ref[s, j : j + 1, :], 0.0) for s in range(4)]
            if j > 0:
                total = total - inward[0] * made[4 * Q : 5 * Q, block(j - 1)]
            if j < EX - 1:
                total = total - inward[1] * made[5 * Q : 6 * Q, block(j + 1)]
            before = pltpu.roll(made[6 * Q : 7 * Q, block(j)], 1, 1)
            after = pltpu.roll(made[7 * Q : 8 * Q, block(j)], EY - 1, 1)
            total = total - jnp.where(lane64 == 0, 0.0, inward[2] * before)
            total = total - jnp.where(lane64 == EY - 1, 0.0, inward[3] * after)
            lim_ref[rows, block(j)] = total
        return 0

    lax.fori_loop(0, F, interior, 0)

    def edges(p):
        first, count, _ = PARTS[p]
        for s in range(4):
            side_copy(p, s).wait_recv()

        def field(f, found):
            found = list(found)
            rows = pl.ds(pl.multiple_of((first + f) * Q, Q), Q)
            made = [
                product(g_ref[(4 + s) * Q : (5 + s) * Q, :], sides[s, rows, :]) for s in range(4)
            ]
            for j in range(EX):
                inward = [jnp.minimum(v_ref[s, j : j + 1, :], 0.0) * gate[s] for s in range(4)]
                total = lim_ref[rows, block(j)]
                if j == 0:
                    total = total - inward[0] * made[0]
                if j == EX - 1:
                    total = total - inward[1] * made[1]
                before = made[2] if j == 0 else pltpu.roll(made[2], EY - j, 1)
                after = pltpu.roll(made[3], EY - 1 - j, 1)
                total = total - jnp.where(lane64 == 0, inward[2] * before, 0.0)
                total = total - jnp.where(lane64 == EY - 1, inward[3] * after, 0.0)
                lim_ref[rows, block(j)] = total
                mean = jnp.sum(total, axis=0, keepdims=True) * (1.0 / Q)
                found[j] = jnp.where(row8 == f, mean, found[j])
            return tuple(found)

        found = lax.fori_loop(
            0, count, field, tuple(jnp.zeros((8, EY), F32) for _ in range(EX))
        )
        low = jnp.zeros((8, EY), F32)
        high = jnp.zeros((8, EY), F32)
        for j in range(EX):
            means[p, :, block(j)] = found[j]
            low = jnp.where(lane8 == j, pltpu.roll(found[j], j, 1) if j else found[j], low)
            high = jnp.where(lane8 == j, pltpu.roll(found[j], j + 1, 1), high)
        mean_packed[p, 0] = low
        mean_packed[p, 1] = high
        for s in range(4):
            mean_copy(p, s).start()

    def limit(p):
        first, count, _ = PARTS[p]
        for s in range(4):
            mean_copy(p, s).wait_recv()
        for j in range(EX):
            center = means[p, :, block(j)]
            if j > 0:
                left = means[p, :, block(j - 1)]
            else:
                left = jnp.where(gate[0] > 0, mean_sides[p, 0], center)
            if j < EX - 1:
                right = means[p, :, block(j + 1)]
            else:
                right = jnp.where(gate[1] > 0, mean_sides[p, 1], center)
            before = mean_sides[p, 2] if j == 0 else pltpu.roll(mean_sides[p, 2], EY - j, 1)
            before = jnp.where(gate[2] > 0, before, center)
            before = jnp.where(lane8 == 0, before, pltpu.roll(center, 1, 1))
            after = pltpu.roll(mean_sides[p, 3], EY - 1 - j, 1)
            after = jnp.where(gate[3] > 0, after, center)
            after = jnp.where(lane8 == EY - 1, after, pltpu.roll(center, EY - 1, 1))
            lower, upper = center, center
            for other in (left, right, before, after):
                lower = jnp.minimum(lower, other)
                upper = jnp.maximum(upper, other)
            lower, upper = lower - MARGIN, upper + MARGIN
            for f in range(count):
                rows = slice((first + f) * Q, (first + f + 1) * Q)
                values = jnp.maximum(lim_ref[rows, block(j)], lower[f : f + 1])
                lim_ref[rows, block(j)] = jnp.minimum(values, upper[f : f + 1])
        for d in (2, 1, 3):
            states_copy(p, d).start()

    edges(0)
    edges(1)
    limit(0)
    edges(2)
    limit(1)
    limit(2)

    table = rank_table(rows_ref)
    for p in range(3):
        axes = PARTS[p][2]
        part_table(table, axes, tables[p])
        at[p][0] = tables[p][here[axes[0]]]
        for d in (2, 1, 3):
            table_copy(p, d).start()

    element = lax.broadcasted_iota(jnp.int32, (E, 256), 0).astype(F32)
    quarter = lax.rem(lax.broadcasted_iota(jnp.int32, (1, 256), 1) // CAP, 4)

    def route(p):
        first, count, axes = PARTS[p]
        rows = count * Q
        me_b = here[axes[1]]
        for d in (0, 1, 3, 2):
            if d:
                states_copy(p, d).wait_recv()
                table_copy(p, d).wait_recv()
            j = (4 - d) % 4
            values = lim_ref[first * Q : first * Q + rows, :] if d == 0 else ar[p][3 - d]
            high, low = halves(values)
            split[j, 0:rows, :] = high
            split[j, rows : 2 * rows, :] = low

        def towards(step, _):
            d = 3 - step
            group = lax.rem(me_b + d, 4) * 2

            def info_of(j, what):
                tile = at[p][j, what]
                lanes = []
                for core in range(2):
                    row = jnp.where(row8 == group + core, tile, 0.0)
                    row = jnp.sum(row, axis=0, keepdims=True)
                    lanes.append(pltpu.roll(row, CAP * j, 1) if j else row)
                return jnp.concatenate(lanes, axis=1)

            infos = []
            for j in range(4):
                infos.append([info_of(j, what) for what in (1, 2, 3)])
                hot = jnp.where(element == info_of(j, 0), 1.0, 0.0).astype(BF16)
                made = jnp.dot(split[j, 0 : 2 * rows, :], hot, preferred_element_type=F32)
                picked[j, 0:rows, :] = made[0:rows] + made[rows:]
            for o in range(4):
                which, slot, weight = infos[3]
                for j in range(3):
                    mine = quarter == (o + j) % 4
                    which = jnp.where(mine, infos[j][0], which)
                    slot = jnp.where(mine, infos[j][1], slot)
                    weight = jnp.where(mine, infos[j][2], weight)
                for f in range(count):
                    part = slice(f * Q, (f + 1) * Q)
                    values = picked[3, part, :]
                    for j in range(3):
                        values = jnp.where(quarter == (o + j) % 4, picked[j, part, :], values)
                    made = product(p_ref[...], values)
                    chosen = made[3 * Q :]
                    for k in range(3):
                        chosen = jnp.where(which == float(k), made[k * Q : (k + 1) * Q], chosen)
                    chosen = chosen * weight
                    bs[p][d, 0, o, part, :] = chosen[:, 0:128]
                    bs[p][d, 1, o, part, :] = chosen[:, 128:256]
                slot = jnp.broadcast_to(slot, (8, 256))
                bs[p][d, 0, o, rows : rows + 8, :] = slot[:, 0:128]
                bs[p][d, 1, o, rows : rows + 8, :] = slot[:, 128:256]
            block_copy(p, d, 1).start()

            @pl.when(d > 0)
            def _():
                block_copy(p, d, 0).start()

            return 0

        lax.fori_loop(0, 4, towards, 0)
        own_copy(p).start()

    def gather(p):
        _, count, axes = PARTS[p]
        rows = count * Q
        me_c = here[axes[2]]
        for number, d in enumerate((0, 1, 3, 2)):
            if d == 0:
                own_copy(p).wait()
                block_copy(p, 0, 1).wait_recv()
            else:
                block_copy(p, d, 0).wait_recv()
                block_copy(p, d, 1).wait_recv()
            slot_of = (4 - d) % 4

            def owner(step, _, number=number, slot_of=slot_of):
                distance = lax.rem(step + 2, 4)
                o = lax.rem(me_c + distance, 4)
                high, low = halves(br[p][slot_of, o, 0:rows, :])
                pair[0:rows, :] = high
                pair[rows : 2 * rows, :] = low
                hot = jnp.where(element == br[p][slot_of, o, rows : rows + 1, :], 1.0, 0.0)
                made = lax.dot_general(
                    pair[0 : 2 * rows, :],
                    hot.astype(BF16),
                    (((1,), (1,)), ((), ())),
                    preferred_element_type=F32,
                )
                total = made[0:rows] + made[rows:]
                if number > 0:
                    total = total + cs[p][o]
                cs[p][o] = total
                if number == 3:

                    @pl.when(distance > 0)
                    def _():
                        sum_copy(p, distance).start()

                return 0

            lax.fori_loop(0, 4, owner, 0)

    def finish(p):
        first, count, axes = PARTS[p]
        total = cs[p][here[axes[2]]]
        for d in (1, 3, 2):
            sum_copy(p, d).wait_recv()
            total = total + cr[p][d - 1]
        out_ref[first * Q : (first + count) * Q, :] = total

    for p in range(3):
        route(p)
    for p in (2, 0, 1):
        gather(p)
    for p in (2, 0, 1):
        finish(p)
    for p in range(3):
        for s in range(4):
            side_copy(p, s).wait_send()
            mean_copy(p, s).wait_send()
        for d in (1, 2, 3):
            states_copy(p, d).wait_send()
            table_copy(p, d).wait_send()
            block_copy(p, d, 0).wait_send()
            block_copy(p, d, 1).wait_send()
            sum_copy(p, d).wait_send()
        block_copy(p, 0, 1).wait_send()


def body(
    states,
    swept_volume,
    flux_own,
    flux_next,
    mass_inverse,
    projection,
    new_owner,
    new_slot,
    intersection_weight,
):
    owner = new_owner.reshape(E, K).T.reshape(E * K)
    slot = new_slot.reshape(E, K).T.reshape(E * K)
    weight = intersection_weight.reshape(E, K).T.reshape(E * K)
    which = jnp.arange(E * K, dtype=jnp.int32)
    element = which % E + 1
    listing = jnp.stack(
        [
            owner.astype(F32),
            (element // 128).astype(F32),
            (element % 128).astype(F32),
            (which // E).astype(F32),
            (slot // 128).astype(F32),
            (slot % 128).astype(F32),
            weight,
            jnp.zeros((E * K,), F32),
        ]
    )
    rows = [count * Q for _, count, _ in PARTS]
    dma = pltpu.SemaphoreType.DMA
    made = pl.pallas_call(
        kernel,
        out_shape=jax.ShapeDtypeStruct((COLS, E), F32),
        in_specs=[VMEM] * 7,
        out_specs=VMEM,
        scratch_shapes=[
            pltpu.VMEM((8 * Q, 3 * Q), BF16),
            pltpu.VMEM((4 * Q, 3 * Q), BF16),
            pltpu.VMEM((COLS, E), F32),
            pltpu.VMEM((4, COLS, EY), F32),
            pltpu.VMEM((2, COLS, EY), F32),
            pltpu.VMEM((3, 8, E), F32),
            pltpu.VMEM((3, 4, 8, EY), F32),
            pltpu.VMEM((3, 2, 8, EY), F32),
        ]
        + [pltpu.VMEM((4, 4, 8, 128), F32) for r in rows]
        + [pltpu.VMEM((3, r, E), F32) for r in rows]
        + [pltpu.VMEM((4, 4, 8, 128), F32) for r in rows]
        + [pltpu.VMEM((4, 2, 4, r + 8, 128), F32) for r in rows]
        + [pltpu.VMEM((4, 4, r + 8, 256), F32) for r in rows]
        + [pltpu.VMEM((4, r, E), F32) for r in rows]
        + [pltpu.VMEM((3, r, E), F32) for r in rows]
        + [
            pltpu.VMEM((4, 2 * max(rows), E), BF16),
            pltpu.VMEM((4, max(rows), 256), F32),
            pltpu.VMEM((2 * max(rows), 256), BF16),
            dma((3, 4)),
            dma((3, 4)),
            dma((3, 4)),
            dma((3, 4)),
            dma((3, 3)),
            dma((3, 3)),
            dma((3, 3)),
            dma((3, 3)),
            dma((3, 4, 2)),
            dma((3, 4, 2)),
            dma((3, 3)),
            dma((3, 3)),
            dma((3,)),
        ],
        compiler_params=pltpu.CompilerParams(
            collective_id=0, has_side_effects=True, vmem_limit_bytes=56 * 2**20
        ),
    )(
        states.reshape(COLS, E),
        swept_volume,
        mass_inverse,
        flux_own,
        flux_next,
        projection,
        listing,
    )
    return made.reshape(F, Q, E)


def solution(mesh):
    placed = (
        P(None, None, "gx", "gy"),
        P(None, "gx", "gy"),
        P(),
        P(),
        P(),
        P(),
        P("gx", "gy", None, None),
        P("gx", "gy", None, None),
        P("gx", "gy", None, None),
    )
    return jax.shard_map(
        body, mesh=mesh, in_specs=placed, out_specs=P(None, None, ("gx", "gy")), check_vma=False
    )
```

```python
import functools

import jax
import jax.numpy as jnp
from jax import lax
from jax.experimental import pallas as pl
from jax.experimental.pallas import tpu as pltpu
from jax.sharding import PartitionSpec as P

F, Q, K, EX, EY, CAP = 8, 64, 4, 4, 128, 32
E = EX * EY
COLS = F * Q
MARGIN = 0.75
MESH = pl.DeviceIdType.MESH
VMEM = pl.BlockSpec(memory_space=pltpu.VMEM)
F32, BF16 = jnp.float32, jnp.bfloat16
PARTS = ((0, 3, "xyz"), (3, 3, "yzx"), (6, 2, "zxy"))


def halves(values):
    high = values.astype(BF16)
    return high, (values - high.astype(F32)).astype(BF16)


def product(matrix, values):
    high, low = halves(values)
    stacked = jnp.concatenate([high, low, high], axis=0)
    return jnp.dot(matrix, stacked, preferred_element_type=F32)


def fold(inverse_ref, sources, target_ref):
    inverse = inverse_ref[...]
    for term, source in enumerate(sources):
        made = jnp.dot(
            inverse, source, precision=lax.Precision.HIGHEST, preferred_element_type=F32
        )
        high, low = halves(made)
        target_ref[term * Q : (term + 1) * Q, :] = jnp.concatenate([high, high, low], axis=1)


def rank_table(rows_ref):
    devices = lax.broadcasted_iota(jnp.int32, (128, 256), 0).astype(F32)
    ranks = lax.broadcasted_iota(jnp.int32, (CAP, 256), 0).astype(F32)
    earlier = lax.broadcasted_iota(jnp.int32, (256, 256), 0) < lax.broadcasted_iota(
        jnp.int32, (256, 256), 1
    )
    earlier = jnp.where(earlier, 1.0, 0.0).astype(BF16)
    carry = jnp.zeros((128, 1), F32)
    table = jnp.zeros((128, 8 * CAP), F32)
    for chunk in range(E * K // 256):
        lanes = slice(chunk * 256, (chunk + 1) * 256)
        named = jnp.where(devices == rows_ref[0:1, lanes], 1.0, 0.0)
        before = jnp.dot(named.astype(BF16), earlier, preferred_element_type=F32) + carry
        rank = jnp.sum(named * before, axis=0, keepdims=True)
        carry = carry + jnp.sum(named, axis=1, keepdims=True)
        placed = ranks == rank
        weight = rows_ref[6:7, lanes]
        first = weight.astype(BF16).astype(F32)
        second = (weight - first).astype(BF16).astype(F32)
        parts = [rows_ref[1 + m : 2 + m, lanes] for m in range(5)]
        parts += [first, second, weight - first - second]
        values = jnp.concatenate([jnp.where(placed, row, 0.0) for row in parts], axis=0)
        table = table + lax.dot_general(
            named.astype(BF16),
            values.astype(BF16),
            (((1,), (1,)), ((), ())),
            preferred_element_type=F32,
        )
    return table.astype(BF16)


STRIDE = {"z": 32, "y": 8, "x": 2}


def part_table(table, axes, target_ref):
    a, b, c = axes
    row = lax.broadcasted_iota(jnp.int32, (32, 128), 0)
    lane = lax.broadcasted_iota(jnp.int32, (32, 128), 1)
    first = (row // 8) * STRIDE[a] + lax.rem(row // 2, 4) * STRIDE[b] + lax.rem(row, 2)
    quarter = lane // CAP
    made = [jnp.zeros((32, 128), F32)] * 8
    for o in range(4):
        chosen = jnp.where(lane == first + o * STRIDE[c], 1.0, 0.0).astype(BF16)
        found = jnp.dot(chosen, table, preferred_element_type=F32)
        for m in range(8):
            tile = found[:, (m // 4) * 128 : (m // 4 + 1) * 128]
            turn = (o - m % 4) % 4
            tile = pltpu.roll(tile, turn * CAP, 1) if turn else tile
            made[m] = jnp.where(quarter == o, tile, made[m])
    whats = (
        made[0] * 128 + made[1] - 1,
        made[2],
        made[3] * 128 + made[4],
        made[5] + made[6] + made[7],
    )
    for place in range(4):
        for number, what in enumerate(whats):
            target_ref[place, number] = what[place * 8 : (place + 1) * 8]


def kernel(
    states_ref, v_ref, inverse_ref, own_ref, next_ref, project_ref, rows_ref, out0, out1, out2,
    u_ref, g_ref, p_ref, lim_ref, sides, packed, means, mean_sides, mean_packed,
    tb0, tb1, tb2, ar0, ar1, ar2, at0, at1, at2, bs0, bs1, bs2, br0, br1, br2,
    cs0, cs1, cs2, cr0, cr1, cr2, ct0, ct1, ct2, split, picked, pair,
    u_sem, h_send, h_recv, m_send, m_recv,
    a_send, a_recv, f_send, f_recv, t_send, t_recv, b_send, b_recv, c_send, c_recv, d_send, d_recv,
    own_sem,
):
    tables, ar, at = (tb0, tb1, tb2), (ar0, ar1, ar2), (at0, at1, at2)
    bs, br, cs, cr = (bs0, bs1, bs2), (br0, br1, br2), (cs0, cs1, cs2), (cr0, cr1, cr2)
    ct, out = (ct0, ct1, ct2), (out0, out1, out2)
    gx, gy = lax.axis_index("gx"), lax.axis_index("gy")
    n_x, n_y = lax.axis_size("gx"), lax.axis_size("gy")
    here = {"x": gy // 2, "y": lax.rem(gx, 4), "z": gx // 4, "c": lax.rem(gy, 2)}
    near = (
        (lax.rem(gx + n_x - 1, n_x), gy),
        (lax.rem(gx + 1, n_x), gy),
        (gx, lax.rem(gy + n_y - 1, n_y)),
        (gx, lax.rem(gy + 1, n_y)),
    )
    inside = (gx > 0, gx < n_x - 1, gy > 0, gy < n_y - 1)
    gate = [jnp.where(there, 1.0, 0.0).astype(F32) for there in inside]

    def away(axis, distance, core=0):
        at_ = dict(here)
        at_[axis] = lax.rem(here[axis] + distance, 4)
        at_["c"] = lax.rem(here["c"] + core, 2)
        return (at_["z"] * 4 + at_["y"], at_["x"] * 2 + at_["c"])

    partners = [away(axis, d, core) for axis in "xyz" for d in (1, 2, 3) for core in (0, 1)]
    partners += [away("x", 0, 1), *near]
    loads = [
        pltpu.make_async_copy(
            states_ref.at[:, j, :], u_ref.at[:, pl.ds(j * EY, EY)], u_sem.at[j]
        )
        for j in range(EX)
    ]
    for load in loads:
        load.start()
    barrier = pltpu.get_barrier_semaphore()
    for device in partners:
        pl.semaphore_signal(barrier, inc=1, device_id=device, device_id_type=MESH)

    def remote(source, target, send, recv, device):
        return pltpu.make_async_remote_copy(
            src_ref=source,
            dst_ref=target,
            send_sem=send,
            recv_sem=recv,
            device_id=device,
            device_id_type=MESH,
        )

    def rows_of(p):
        first, count, _ = PARTS[p]
        return pl.ds(first * Q, count * Q)

    def side_copy(p, s):
        rows = rows_of(p)
        source = (
            u_ref.at[rows, pl.ds(0, EY)],
            u_ref.at[rows, pl.ds(3 * EY, EY)],
            packed.at[0, rows],
            packed.at[1, rows],
        )[s]
        return remote(
            source, sides.at[s ^ 1, rows], h_send.at[p, s], h_recv.at[p, s ^ 1], near[s]
        )

    def mean_copy(p, s):
        source = (
            means.at[p, :, pl.ds(0, EY)],
            means.at[p, :, pl.ds(3 * EY, EY)],
            mean_packed.at[p, 0],
            mean_packed.at[p, 1],
        )[s]
        return remote(
            source, mean_sides.at[p, s ^ 1], m_send.at[p, s], m_recv.at[p, s ^ 1], near[s]
        )

    def half_of(p, h):
        size = PARTS[p][1] * Q // 2
        return pl.ds(h * size, size)

    def states_copy(p, d, h):
        first, count, axes = PARTS[p]
        size = count * Q // 2
        return remote(
            lim_ref.at[pl.ds(first * Q + h * size, size)],
            ar[p].at[3 - d, half_of(p, h)],
            a_send.at[p, d // 2, h],
            a_recv.at[p, d // 2, h],
            away(axes[0], d),
        )

    def relay_copy(p, d):
        half = half_of(p, d // 2)
        return remote(
            ar[p].at[3 - d, half],
            ar[p].at[1, half],
            f_send.at[p, d // 2],
            f_recv.at[p, d // 2],
            away(PARTS[p][2][0], d),
        )

    def table_copy(p, d):
        axis = PARTS[p][2][0]
        return remote(
            tables[p].at[lax.rem(here[axis] + d, 4)],
            at[p].at[4 - d],
            t_send.at[p, d - 1],
            t_recv.at[p, d - 1],
            away(axis, d),
        )

    def block_copy(p, d, core):
        return remote(
            bs[p].at[d, lax.rem(here["c"] + core, 2)],
            br[p].at[lax.rem(4 - d, 4), :, pl.ds(core * 128, 128)],
            b_send.at[p, d, core],
            b_recv.at[p, d, core],
            away(PARTS[p][2][1], d, core),
        )

    def own_copy(p):
        return pltpu.make_async_copy(
            bs[p].at[0, here["c"]], br[p].at[0, :, pl.ds(0, 128)], own_sem.at[p]
        )

    def owner_at(p, d):
        return lax.rem(here[PARTS[p][2][2]] + d, 4)

    def far_sum(p, d):
        return remote(
            cs[p].at[owner_at(p, 2), half_of(p, d // 2)],
            ct[p].at[d // 2],
            d_send.at[p, d // 2],
            d_recv.at[p, d // 2],
            away(PARTS[p][2][2], d),
        )

    def near_sum(p, d, h):
        half = half_of(p, h)
        return remote(
            cs[p].at[owner_at(p, d), half],
            cr[p].at[d // 2, half],
            c_send.at[p, d // 2, h],
            c_recv.at[p, d // 2, h],
            away(PARTS[p][2][2], d),
        )

    lane64 = lax.broadcasted_iota(jnp.int32, (Q, EY), 1)
    lane8 = lax.broadcasted_iota(jnp.int32, (8, EY), 1)
    row8 = lax.broadcasted_iota(jnp.int32, (8, EY), 0)
    row256 = lax.broadcasted_iota(jnp.int32, (8, 256), 0)

    def block(j):
        return slice(j * EY, (j + 1) * EY)

    def pack(f, _):
        rows = pl.ds(pl.multiple_of(f * Q, Q), Q)
        low = jnp.zeros((Q, EY), F32)
        high = jnp.zeros((Q, EY), F32)
        for j in range(EX):
            values = u_ref[rows, block(j)]
            low = jnp.where(lane64 == j, pltpu.roll(values, j, 1) if j else values, low)
            high = jnp.where(lane64 == j, pltpu.roll(values, j + 1, 1), high)
        packed[0, rows, :] = low
        packed[1, rows, :] = high
        return 0

    for load in loads:
        load.wait()
    lax.fori_loop(0, F, pack, 0)
    pl.semaphore_wait(barrier, len(partners))
    for p in range(3):
        for s in range(4):
            side_copy(p, s).start()
    fold(inverse_ref, [own_ref[s] for s in range(4)] + [next_ref[s] for s in range(4)], g_ref)
    fold(inverse_ref, [project_ref[k] for k in range(4)], p_ref)

    def interior(f, _):
        rows = pl.ds(pl.multiple_of(f * Q, Q), Q)
        u = u_ref[rows, :]
        made = product(g_ref[...], u)
        for j in range(EX):
            total = u[:, block(j)]
            for s in range(4):
                outward = jnp.maximum(v_ref[s, j : j + 1, :], 0.0)
                total = total - outward * made[s * Q : (s + 1) * Q, block(j)]
            inward = [jnp.minimum(v_ref[s, j : j + 1, :], 0.0) for s in range(4)]
            if j > 0:
                total = total - inward[0] * made[4 * Q : 5 * Q, block(j - 1)]
            if j < EX - 1:
                total = total - inward[1] * made[5 * Q : 6 * Q, block(j + 1)]
            before = pltpu.roll(made[6 * Q : 7 * Q, block(j)], 1, 1)
            after = pltpu.roll(made[7 * Q : 8 * Q, block(j)], EY - 1, 1)
            total = total - jnp.where(lane64 == 0, 0.0, inward[2] * before)
            total = total - jnp.where(lane64 == EY - 1, 0.0, inward[3] * after)
            lim_ref[rows, block(j)] = total
        return 0

    lax.fori_loop(0, F, interior, 0)

    def edges(p):
        first, count, _ = PARTS[p]
        for s in range(4):
            side_copy(p, s).wait_recv()

        def field(f, found):
            found = list(found)
            rows = pl.ds(pl.multiple_of((first + f) * Q, Q), Q)
            made = [
                product(g_ref[(4 + s) * Q : (5 + s) * Q, :], sides[s, rows, :]) for s in range(4)
            ]
            for j in range(EX):
                inward = [jnp.minimum(v_ref[s, j : j + 1, :], 0.0) * gate[s] for s in range(4)]
                total = lim_ref[rows, block(j)]
                if j == 0:
                    total = total - inward[0] * made[0]
                if j == EX - 1:
                    total = total - inward[1] * made[1]
                before = made[2] if j == 0 else pltpu.roll(made[2], EY - j, 1)
                after = pltpu.roll(made[3], EY - 1 - j, 1)
                total = total - jnp.where(lane64 == 0, inward[2] * before, 0.0)
                total = total - jnp.where(lane64 == EY - 1, inward[3] * after, 0.0)
                lim_ref[rows, block(j)] = total
                mean = jnp.sum(total, axis=0, keepdims=True) * (1.0 / Q)
                found[j] = jnp.where(row8 == f, mean, found[j])
            return tuple(found)

        found = lax.fori_loop(
            0, count, field, tuple(jnp.zeros((8, EY), F32) for _ in range(EX))
        )
        low = jnp.zeros((8, EY), F32)
        high = jnp.zeros((8, EY), F32)
        for j in range(EX):
            means[p, :, block(j)] = found[j]
            low = jnp.where(lane8 == j, pltpu.roll(found[j], j, 1) if j else found[j], low)
            high = jnp.where(lane8 == j, pltpu.roll(found[j], j + 1, 1), high)
        mean_packed[p, 0] = low
        mean_packed[p, 1] = high
        for s in range(4):
            mean_copy(p, s).start()

    def limit(p):
        first, count, _ = PARTS[p]
        for s in range(4):
            mean_copy(p, s).wait_recv()
        for j in range(EX):
            center = means[p, :, block(j)]
            if j > 0:
                left = means[p, :, block(j - 1)]
            else:
                left = jnp.where(gate[0] > 0, mean_sides[p, 0], center)
            if j < EX - 1:
                right = means[p, :, block(j + 1)]
            else:
                right = jnp.where(gate[1] > 0, mean_sides[p, 1], center)
            before = mean_sides[p, 2] if j == 0 else pltpu.roll(mean_sides[p, 2], EY - j, 1)
            before = jnp.where(gate[2] > 0, before, center)
            before = jnp.where(lane8 == 0, before, pltpu.roll(center, 1, 1))
            after = pltpu.roll(mean_sides[p, 3], EY - 1 - j, 1)
            after = jnp.where(gate[3] > 0, after, center)
            after = jnp.where(lane8 == EY - 1, after, pltpu.roll(center, EY - 1, 1))
            lower, upper = center, center
            for other in (left, right, before, after):
                lower = jnp.minimum(lower, other)
                upper = jnp.maximum(upper, other)
            lower, upper = lower - MARGIN, upper + MARGIN
            for f in range(count):
                rows = slice((first + f) * Q, (first + f + 1) * Q)
                values = jnp.maximum(lim_ref[rows, block(j)], lower[f : f + 1])
                lim_ref[rows, block(j)] = jnp.minimum(values, upper[f : f + 1])
        for h in (0, 1):
            states_copy(p, 1, h).start()
            states_copy(p, 3, 1 - h).start()

    for p in range(3):
        edges(p)
    for p in range(3):
        limit(p)

    table = rank_table(rows_ref)
    for p in range(3):
        axes = PARTS[p][2]
        part_table(table, axes, tables[p])
        at[p][0] = tables[p][here[axes[0]]]
        for d in (2, 1, 3):
            table_copy(p, d).start()
    for p in range(3):
        for d in (1, 3):
            states_copy(p, d, d // 2).wait_recv()
            relay_copy(p, d).start()

    element = lax.broadcasted_iota(jnp.int32, (E, 256), 0).astype(F32)
    quarter = lax.rem(lax.broadcasted_iota(jnp.int32, (1, 256), 1) // CAP, 4)

    def route(p):
        first, count, axes = PARTS[p]
        rows = count * Q
        me_b = here[axes[1]]
        for d in (0, 1, 3, 2):
            if d:
                table_copy(p, d).wait_recv()
            if d == 2:
                relay_copy(p, 1).wait_recv()
                relay_copy(p, 3).wait_recv()
            elif d:
                states_copy(p, d, 1 - d // 2).wait_recv()
            j = (4 - d) % 4
            values = lim_ref[first * Q : first * Q + rows, :] if d == 0 else ar[p][3 - d]
            high, low = halves(values)
            split[j, 0:rows, :] = high
            split[j, rows : 2 * rows, :] = low

        def towards(step, _):
            d = 3 - step
            group = lax.rem(me_b + d, 4) * 2

            def info_of(j, what):
                tile = at[p][j, what]
                lanes = []
                for core in range(2):
                    row = jnp.where(row8 == group + core, tile, 0.0)
                    row = jnp.sum(row, axis=0, keepdims=True)
                    lanes.append(pltpu.roll(row, CAP * j, 1) if j else row)
                return jnp.concatenate(lanes, axis=1)

            infos = []
            for j in range(4):
                infos.append([info_of(j, what) for what in (1, 2, 3)])
                hot = jnp.where(element == info_of(j, 0), 1.0, 0.0).astype(BF16)
                made = jnp.dot(split[j, 0 : 2 * rows, :], hot, preferred_element_type=F32)
                picked[j, 0:rows, :] = made[0:rows] + made[rows:]
            slots = jnp.zeros((8, 256), F32)
            for o in range(4):
                which, slot, weight = infos[3]
                for j in range(3):
                    mine = quarter == (o + j) % 4
                    which = jnp.where(mine, infos[j][0], which)
                    slot = jnp.where(mine, infos[j][1], slot)
                    weight = jnp.where(mine, infos[j][2], weight)
                for f in range(count):
                    part = slice(f * Q, (f + 1) * Q)
                    values = picked[3, part, :]
                    for j in range(3):
                        values = jnp.where(quarter == (o + j) % 4, picked[j, part, :], values)
                    made = product(p_ref[...], values)
                    chosen = made[3 * Q :]
                    for k in range(3):
                        chosen = jnp.where(which == float(k), made[k * Q : (k + 1) * Q], chosen)
                    chosen = chosen * weight
                    place = slice(o * rows + f * Q, o * rows + (f + 1) * Q)
                    bs[p][d, 0, place, :] = chosen[:, 0:128]
                    bs[p][d, 1, place, :] = chosen[:, 128:256]
                slots = jnp.where(row256 == o, slot, slots)
            bs[p][d, 0, 4 * rows : 4 * rows + 8, :] = slots[:, 0:128]
            bs[p][d, 1, 4 * rows : 4 * rows + 8, :] = slots[:, 128:256]
            block_copy(p, d, 1).start()

            @pl.when(d > 0)
            def _():
                block_copy(p, d, 0).start()

            return 0

        lax.fori_loop(0, 4, towards, 0)
        own_copy(p).start()

    def gather(p):
        _, count, axes = PARTS[p]
        rows = count * Q
        me_c = here[axes[2]]
        for number, d in enumerate((0, 1, 3, 2)):
            if d == 0:
                own_copy(p).wait()
                block_copy(p, 0, 1).wait_recv()
            else:
                block_copy(p, d, 0).wait_recv()
                block_copy(p, d, 1).wait_recv()
            slot_of = (4 - d) % 4

            def owner(distance, number=number, slot_of=slot_of):
                o = lax.rem(me_c + distance, 4)
                place = pl.ds(pl.multiple_of(o * rows, rows), rows)
                high, low = halves(br[p][slot_of, place, :])
                pair[0:rows, :] = high
                pair[rows : 2 * rows, :] = low
                slot = br[p][slot_of, 4 * rows : 4 * rows + 8, :]
                slot = jnp.sum(jnp.where(row256 == o, slot, 0.0), axis=0, keepdims=True)
                hot = jnp.where(element == slot, 1.0, 0.0)
                made = lax.dot_general(
                    pair[0 : 2 * rows, :],
                    hot.astype(BF16),
                    (((1,), (1,)), ((), ())),
                    preferred_element_type=F32,
                )
                total = made[0:rows] + made[rows:]
                if number > 0:
                    total = total + cs[p][o]
                cs[p][o] = total

            if number < 3:

                def step(distance, _, owner=owner):
                    owner(distance)
                    return 0

                lax.fori_loop(0, 4, step, 0)
            else:
                owner(2)
                far_sum(p, 1).start()
                far_sum(p, 3).start()
                owner(1)
                near_sum(p, 1, 1).start()
                owner(3)
                near_sum(p, 3, 0).start()
                owner(0)

    def combine(p):
        half = PARTS[p][1] * Q // 2
        for d in (1, 3):
            far_sum(p, d).wait_recv()
            o = owner_at(p, d)
            place = slice((d // 2) * half, (d // 2 + 1) * half)
            cs[p][o, place, :] = cs[p][o, place, :] + ct[p][d // 2]
            near_sum(p, d, d // 2).start()

    def finish(p):
        total = cs[p][here[PARTS[p][2][2]]]
        for d in (1, 3):
            for h in (0, 1):
                near_sum(p, d, h).wait_recv()
            total = total + cr[p][d // 2]
        out[p][...] = total

    for p in range(3):
        route(p)
    gather(2)
    combine(2)
    gather(0)
    gather(1)
    for p in (0, 1):
        combine(p)
    for p in (2, 0, 1):
        finish(p)
    for p in range(3):
        for s in range(4):
            side_copy(p, s).wait_send()
            mean_copy(p, s).wait_send()
        for d in (1, 3):
            for h in (0, 1):
                states_copy(p, d, h).wait_send()
                near_sum(p, d, h).wait_send()
            relay_copy(p, d).wait_send()
            far_sum(p, d).wait_send()
        for d in (1, 2, 3):
            table_copy(p, d).wait_send()
            block_copy(p, d, 0).wait_send()
            block_copy(p, d, 1).wait_send()
        block_copy(p, 0, 1).wait_send()


def body(
    states,
    swept_volume,
    flux_own,
    flux_next,
    mass_inverse,
    projection,
    new_owner,
    new_slot,
    intersection_weight,
):
    owner = new_owner.reshape(E, K).T.reshape(E * K)
    slot = new_slot.reshape(E, K).T.reshape(E * K)
    weight = intersection_weight.reshape(E, K).T.reshape(E * K)
    which = jnp.arange(E * K, dtype=jnp.int32)
    element = which % E + 1
    listing = jnp.stack(
        [
            owner.astype(F32),
            (element // 128).astype(F32),
            (element % 128).astype(F32),
            (which // E).astype(F32),
            (slot // 128).astype(F32),
            (slot % 128).astype(F32),
            weight,
            jnp.zeros((E * K,), F32),
        ]
    )
    rows = [count * Q for _, count, _ in PARTS]
    dma = pltpu.SemaphoreType.DMA
    made = pl.pallas_call(
        kernel,
        out_shape=[jax.ShapeDtypeStruct((r, E), F32) for r in rows],
        in_specs=[pl.BlockSpec(memory_space=pl.ANY)] + [VMEM] * 6,
        out_specs=[VMEM] * 3,
        scratch_shapes=[
            pltpu.VMEM((COLS, E), F32),
            pltpu.VMEM((8 * Q, 3 * Q), BF16),
            pltpu.VMEM((4 * Q, 3 * Q), BF16),
            pltpu.VMEM((COLS, E), F32),
            pltpu.VMEM((4, COLS, EY), F32),
            pltpu.VMEM((2, COLS, EY), F32),
            pltpu.VMEM((3, 8, E), F32),
            pltpu.VMEM((3, 4, 8, EY), F32),
            pltpu.VMEM((3, 2, 8, EY), F32),
        ]
        + [pltpu.VMEM((4, 4, 8, 128), F32) for r in rows]
        + [pltpu.VMEM((3, r, E), F32) for r in rows]
        + [pltpu.VMEM((4, 4, 8, 128), F32) for r in rows]
        + [pltpu.VMEM((4, 2, 4 * r + 8, 128), F32) for r in rows]
        + [pltpu.VMEM((4, 4 * r + 8, 256), F32) for r in rows]
        + [pltpu.VMEM((4, r, E), F32) for r in rows]
        + [pltpu.VMEM((2, r, E), F32) for r in rows]
        + [pltpu.VMEM((2, r // 2, E), F32) for r in rows]
        + [
            pltpu.VMEM((4, 2 * max(rows), E), BF16),
            pltpu.VMEM((4, max(rows), 256), F32),
            pltpu.VMEM((2 * max(rows), 256), BF16),
            dma((4,)),
            *[dma((3, 4))] * 4,
            *[dma((3, 2, 2))] * 2,
            *[dma((3, 2))] * 2,
            *[dma((3, 3))] * 2,
            *[dma((3, 4, 2))] * 2,
            *[dma((3, 2, 2))] * 2,
            *[dma((3, 2))] * 2,
            dma((3,)),
        ],
        compiler_params=pltpu.CompilerParams(
            collective_id=0, has_side_effects=True, vmem_limit_bytes=56 * 2**20
        ),
    )(
        states.reshape(COLS, EX, EY),
        swept_volume,
        mass_inverse,
        flux_own,
        flux_next,
        projection,
        listing,
    )
    return jnp.concatenate(made, axis=0).reshape(F, Q, E)


def solution(mesh):
    placed = (
        P(None, None, "gx", "gy"),
        P(None, "gx", "gy"),
        P(),
        P(),
        P(),
        P(),
        P("gx", "gy", None, None),
        P("gx", "gy", None, None),
        P("gx", "gy", None, None),
    )
    return jax.shard_map(
        body, mesh=mesh, in_specs=placed, out_specs=P(None, None, ("gx", "gy")), check_vma=False
    )
```

```python
import functools

import jax
import jax.numpy as jnp
from jax import lax
from jax.experimental import pallas as pl
from jax.experimental.pallas import tpu as pltpu
from jax.sharding import PartitionSpec as P

F, Q, K, EX, EY, CAP = 8, 64, 4, 4, 128, 32
E = EX * EY
COLS = F * Q
MARGIN = 0.75
MESH = pl.DeviceIdType.MESH
VMEM = pl.BlockSpec(memory_space=pltpu.VMEM)
HBM = pl.BlockSpec(memory_space=pltpu.HBM)
F32, BF16 = jnp.float32, jnp.bfloat16
PARTS = ((0, 3, "xyz"), (3, 3, "yzx"), (6, 2, "zxy"))


def halves(values):
    high = values.astype(BF16)
    return high, (values - high.astype(F32)).astype(BF16)


def product(matrix, values):
    high, low = halves(values)
    stacked = jnp.concatenate([high, low, high], axis=0)
    return jnp.dot(matrix, stacked, preferred_element_type=F32)


def fold(inverse_ref, sources, target_ref):
    inverse = inverse_ref[...]
    for term, source in enumerate(sources):
        made = jnp.dot(
            inverse, source, precision=lax.Precision.HIGHEST, preferred_element_type=F32
        )
        high, low = halves(made)
        target_ref[term * Q : (term + 1) * Q, :] = jnp.concatenate([high, high, low], axis=1)


def rank_table(owner_ref, slot_ref, weight_ref):
    devices = lax.broadcasted_iota(jnp.int32, (128, 256), 0)
    ranks = lax.broadcasted_iota(jnp.int32, (CAP, 256), 0).astype(F32)
    earlier = lax.broadcasted_iota(jnp.int32, (256, 256), 0) < lax.broadcasted_iota(
        jnp.int32, (256, 256), 1
    )
    earlier = jnp.where(earlier, 1.0, 0.0).astype(BF16)
    carry = jnp.zeros((128, 1), F32)
    table = jnp.zeros((128, 8 * CAP), F32)
    for k in range(K):
        for start in range(0, E, 256):
            lanes = slice(start, start + 256)
            named = jnp.where(devices == owner_ref[k : k + 1, lanes], 1.0, 0.0)
            before = jnp.dot(named.astype(BF16), earlier, preferred_element_type=F32) + carry
            rank = jnp.sum(named * before, axis=0, keepdims=True)
            carry = carry + jnp.sum(named, axis=1, keepdims=True)
            placed = ranks == rank
            weight = weight_ref[k : k + 1, lanes]
            first = weight.astype(BF16).astype(F32)
            second = (weight - first).astype(BF16).astype(F32)
            slot = slot_ref[k : k + 1, lanes]
            element = lax.broadcasted_iota(jnp.int32, (1, 256), 1) + (start + 1)
            parts = [
                (element // 128).astype(F32),
                lax.rem(element, 128).astype(F32),
                jnp.full((1, 256), float(k), F32),
                (slot // 128).astype(F32),
                lax.rem(slot, 128).astype(F32),
                first,
                second,
                weight - first - second,
            ]
            values = jnp.concatenate([jnp.where(placed, row, 0.0) for row in parts], axis=0)
            table = table + lax.dot_general(
                named.astype(BF16),
                values.astype(BF16),
                (((1,), (1,)), ((), ())),
                preferred_element_type=F32,
            )
    return table.astype(BF16)


STRIDE = {"z": 32, "y": 8, "x": 2}


def part_table(table, axes, target_ref):
    a, b, c = axes
    row = lax.broadcasted_iota(jnp.int32, (32, 128), 0)
    lane = lax.broadcasted_iota(jnp.int32, (32, 128), 1)
    first = (row // 8) * STRIDE[a] + lax.rem(row // 2, 4) * STRIDE[b] + lax.rem(row, 2)
    quarter = lane // CAP
    made = [jnp.zeros((32, 128), F32)] * 8
    for o in range(4):
        chosen = jnp.where(lane == first + o * STRIDE[c], 1.0, 0.0).astype(BF16)
        found = jnp.dot(chosen, table, preferred_element_type=F32)
        for m in range(8):
            tile = found[:, (m // 4) * 128 : (m // 4 + 1) * 128]
            turn = (o - m % 4) % 4
            tile = pltpu.roll(tile, turn * CAP, 1) if turn else tile
            made[m] = jnp.where(quarter == o, tile, made[m])
    whats = (
        made[0] * 128 + made[1] - 1,
        made[2],
        made[3] * 128 + made[4],
        made[5] + made[6] + made[7],
    )
    for place in range(4):
        for number, what in enumerate(whats):
            target_ref[place, number] = what[place * 8 : (place + 1) * 8]


def kernel(
    states_ref, v_ref, inverse_ref, own_ref, next_ref, project_ref,
    owner_hbm, slot_hbm, weight_hbm, out0, out1, out2, owner_ref, slot_ref, weight_ref, u_ref, g_ref, p_ref, lim_ref, sides, packed, means, mean_sides, mean_packed,
    tb0, tb1, tb2, ar0, ar1, ar2, at0, at1, at2, bs0, bs1, bs2, br0, br1, br2,
    cs0, cs1, cs2, cr0, cr1, cr2, ct0, ct1, ct2, sp0, sp1, sp2, picked, pair,
    u_sem, h_send, h_recv, m_send, m_recv,
    a_send, a_recv, f_send, f_recv, t_send, t_recv, b_send, b_recv, c_send, c_recv, d_send, d_recv,
    own_sem,
):
    tables, ar, at = (tb0, tb1, tb2), (ar0, ar1, ar2), (at0, at1, at2)
    bs, br, cs, cr = (bs0, bs1, bs2), (br0, br1, br2), (cs0, cs1, cs2), (cr0, cr1, cr2)
    ct, out = (ct0, ct1, ct2), (out0, out1, out2)
    gx, gy = lax.axis_index("gx"), lax.axis_index("gy")
    n_x, n_y = lax.axis_size("gx"), lax.axis_size("gy")
    here = {"x": gy // 2, "y": lax.rem(gx, 4), "z": gx // 4, "c": lax.rem(gy, 2)}
    near = (
        (lax.rem(gx + n_x - 1, n_x), gy),
        (lax.rem(gx + 1, n_x), gy),
        (gx, lax.rem(gy + n_y - 1, n_y)),
        (gx, lax.rem(gy + 1, n_y)),
    )
    inside = (gx > 0, gx < n_x - 1, gy > 0, gy < n_y - 1)
    gate = [jnp.where(there, 1.0, 0.0).astype(F32) for there in inside]

    def away(axis, distance, core=0):
        at_ = dict(here)
        at_[axis] = lax.rem(here[axis] + distance, 4)
        at_["c"] = lax.rem(here["c"] + core, 2)
        return (at_["z"] * 4 + at_["y"], at_["x"] * 2 + at_["c"])

    partners = [away(axis, d, core) for axis in "xyz" for d in (1, 2, 3) for core in (0, 1)]
    partners += [away("x", 0, 1), *near]
    loads = [
        pltpu.make_async_copy(
            states_ref.at[:, j, :], u_ref.at[:, pl.ds(j * EY, EY)], u_sem.at[j]
        )
        for j in range(EX)
    ]
    lists = [
        pltpu.make_async_copy(source, target, u_sem.at[EX + i])
        for i, (source, target) in enumerate(
            ((owner_hbm, owner_ref), (slot_hbm, slot_ref), (weight_hbm, weight_ref))
        )
    ]
    for load in loads + lists:
        load.start()
    barrier = pltpu.get_barrier_semaphore()
    for device in partners:
        pl.semaphore_signal(barrier, inc=1, device_id=device, device_id_type=MESH)

    def remote(source, target, send, recv, device):
        return pltpu.make_async_remote_copy(
            src_ref=source,
            dst_ref=target,
            send_sem=send,
            recv_sem=recv,
            device_id=device,
            device_id_type=MESH,
        )

    def rows_of(p):
        first, count, _ = PARTS[p]
        return pl.ds(first * Q, count * Q)

    def side_copy(p, s):
        rows = rows_of(p)
        source = (
            u_ref.at[rows, pl.ds(0, EY)],
            u_ref.at[rows, pl.ds(3 * EY, EY)],
            packed.at[0, rows],
            packed.at[1, rows],
        )[s]
        return remote(
            source, sides.at[s ^ 1, rows], h_send.at[p, s], h_recv.at[p, s ^ 1], near[s]
        )

    def mean_copy(p, s):
        source = (
            means.at[p, :, pl.ds(0, EY)],
            means.at[p, :, pl.ds(3 * EY, EY)],
            mean_packed.at[p, 0],
            mean_packed.at[p, 1],
        )[s]
        return remote(
            source, mean_sides.at[p, s ^ 1], m_send.at[p, s], m_recv.at[p, s ^ 1], near[s]
        )

    def half_of(p, h):
        size = PARTS[p][1] * Q // 2
        return pl.ds(h * size, size)

    def states_copy(p, d, h):
        first, count, axes = PARTS[p]
        size = count * Q // 2
        return remote(
            lim_ref.at[pl.ds(first * Q + h * size, size)],
            ar[p].at[3 - d, half_of(p, h)],
            a_send.at[p, d // 2, h],
            a_recv.at[p, d // 2, h],
            away(axes[0], d),
        )

    def relay_copy(p, d):
        half = half_of(p, d // 2)
        return remote(
            ar[p].at[3 - d, half],
            ar[p].at[1, half],
            f_send.at[p, d // 2],
            f_recv.at[p, d // 2],
            away(PARTS[p][2][0], d),
        )

    def table_copy(p, d):
        axis = PARTS[p][2][0]
        return remote(
            tables[p].at[lax.rem(here[axis] + d, 4)],
            at[p].at[4 - d],
            t_send.at[p, d - 1],
            t_recv.at[p, d - 1],
            away(axis, d),
        )

    def block_copy(p, d, core):
        return remote(
            bs[p].at[d, lax.rem(here["c"] + core, 2)],
            br[p].at[lax.rem(4 - d, 4), :, pl.ds(core * 128, 128)],
            b_send.at[p, d, core],
            b_recv.at[p, d, core],
            away(PARTS[p][2][1], d, core),
        )

    def own_copy(p):
        return pltpu.make_async_copy(
            bs[p].at[0, here["c"]], br[p].at[0, :, pl.ds(0, 128)], own_sem.at[p]
        )

    def owner_at(p, d):
        return lax.rem(here[PARTS[p][2][2]] + d, 4)

    def far_sum(p, d):
        return remote(
            cs[p].at[owner_at(p, 2), half_of(p, d // 2)],
            ct[p].at[d // 2],
            d_send.at[p, d // 2],
            d_recv.at[p, d // 2],
            away(PARTS[p][2][2], d),
        )

    def near_sum(p, d, h):
        half = half_of(p, h)
        return remote(
            cs[p].at[owner_at(p, d), half],
            cr[p].at[d // 2, half],
            c_send.at[p, d // 2, h],
            c_recv.at[p, d // 2, h],
            away(PARTS[p][2][2], d),
        )

    lane64 = lax.broadcasted_iota(jnp.int32, (Q, EY), 1)
    lane8 = lax.broadcasted_iota(jnp.int32, (8, EY), 1)
    row8 = lax.broadcasted_iota(jnp.int32, (8, EY), 0)
    row256 = lax.broadcasted_iota(jnp.int32, (8, 256), 0)

    def block(j):
        return slice(j * EY, (j + 1) * EY)

    def pack(f, _):
        rows = pl.ds(pl.multiple_of(f * Q, Q), Q)
        low = jnp.zeros((Q, EY), F32)
        high = jnp.zeros((Q, EY), F32)
        for j in range(EX):
            values = u_ref[rows, block(j)]
            low = jnp.where(lane64 == j, pltpu.roll(values, j, 1) if j else values, low)
            high = jnp.where(lane64 == j, pltpu.roll(values, j + 1, 1), high)
        packed[0, rows, :] = low
        packed[1, rows, :] = high
        return 0

    for load in loads + lists:
        load.wait()
    lax.fori_loop(0, F, pack, 0)
    pl.semaphore_wait(barrier, len(partners))
    for p in range(3):
        for s in range(4):
            side_copy(p, s).start()
    fold(inverse_ref, [own_ref[s] for s in range(4)] + [next_ref[s] for s in range(4)], g_ref)
    fold(inverse_ref, [project_ref[k] for k in range(4)], p_ref)

    def interior(f, _):
        rows = pl.ds(pl.multiple_of(f * Q, Q), Q)
        u = u_ref[rows, :]
        made = product(g_ref[...], u)
        for j in range(EX):
            total = u[:, block(j)]
            for s in range(4):
                outward = jnp.maximum(v_ref[s, j : j + 1, :], 0.0)
                total = total - outward * made[s * Q : (s + 1) * Q, block(j)]
            inward = [jnp.minimum(v_ref[s, j : j + 1, :], 0.0) for s in range(4)]
            if j > 0:
                total = total - inward[0] * made[4 * Q : 5 * Q, block(j - 1)]
            if j < EX - 1:
                total = total - inward[1] * made[5 * Q : 6 * Q, block(j + 1)]
            before = pltpu.roll(made[6 * Q : 7 * Q, block(j)], 1, 1)
            after = pltpu.roll(made[7 * Q : 8 * Q, block(j)], EY - 1, 1)
            total = total - jnp.where(lane64 == 0, 0.0, inward[2] * before)
            total = total - jnp.where(lane64 == EY - 1, 0.0, inward[3] * after)
            lim_ref[rows, block(j)] = total
        return 0

    lax.fori_loop(0, F, interior, 0)

    def edges(p):
        first, count, _ = PARTS[p]
        for s in range(4):
            side_copy(p, s).wait_recv()

        def field(f, found):
            found = list(found)
            rows = pl.ds(pl.multiple_of((first + f) * Q, Q), Q)
            made = [
                product(g_ref[(4 + s) * Q : (5 + s) * Q, :], sides[s, rows, :]) for s in range(4)
            ]
            for j in range(EX):
                inward = [jnp.minimum(v_ref[s, j : j + 1, :], 0.0) * gate[s] for s in range(4)]
                total = lim_ref[rows, block(j)]
                if j == 0:
                    total = total - inward[0] * made[0]
                if j == EX - 1:
                    total = total - inward[1] * made[1]
                before = made[2] if j == 0 else pltpu.roll(made[2], EY - j, 1)
                after = pltpu.roll(made[3], EY - 1 - j, 1)
                total = total - jnp.where(lane64 == 0, inward[2] * before, 0.0)
                total = total - jnp.where(lane64 == EY - 1, inward[3] * after, 0.0)
                lim_ref[rows, block(j)] = total
                mean = jnp.sum(total, axis=0, keepdims=True) * (1.0 / Q)
                found[j] = jnp.where(row8 == f, mean, found[j])
            return tuple(found)

        found = lax.fori_loop(
            0, count, field, tuple(jnp.zeros((8, EY), F32) for _ in range(EX))
        )
        low = jnp.zeros((8, EY), F32)
        high = jnp.zeros((8, EY), F32)
        for j in range(EX):
            means[p, :, block(j)] = found[j]
            low = jnp.where(lane8 == j, pltpu.roll(found[j], j, 1) if j else found[j], low)
            high = jnp.where(lane8 == j, pltpu.roll(found[j], j + 1, 1), high)
        mean_packed[p, 0] = low
        mean_packed[p, 1] = high
        for s in range(4):
            mean_copy(p, s).start()

    def limit(p):
        first, count, _ = PARTS[p]
        for s in range(4):
            mean_copy(p, s).wait_recv()
        for j in range(EX):
            center = means[p, :, block(j)]
            if j > 0:
                left = means[p, :, block(j - 1)]
            else:
                left = jnp.where(gate[0] > 0, mean_sides[p, 0], center)
            if j < EX - 1:
                right = means[p, :, block(j + 1)]
            else:
                right = jnp.where(gate[1] > 0, mean_sides[p, 1], center)
            before = mean_sides[p, 2] if j == 0 else pltpu.roll(mean_sides[p, 2], EY - j, 1)
            before = jnp.where(gate[2] > 0, before, center)
            before = jnp.where(lane8 == 0, before, pltpu.roll(center, 1, 1))
            after = pltpu.roll(mean_sides[p, 3], EY - 1 - j, 1)
            after = jnp.where(gate[3] > 0, after, center)
            after = jnp.where(lane8 == EY - 1, after, pltpu.roll(center, EY - 1, 1))
            lower, upper = center, center
            for other in (left, right, before, after):
                lower = jnp.minimum(lower, other)
                upper = jnp.maximum(upper, other)
            lower, upper = lower - MARGIN, upper + MARGIN
            for f in range(count):
                rows = slice((first + f) * Q, (first + f + 1) * Q)
                values = jnp.maximum(lim_ref[rows, block(j)], lower[f : f + 1])
                lim_ref[rows, block(j)] = jnp.minimum(values, upper[f : f + 1])
        states_copy(p, 1, 0).start()
        states_copy(p, 3, 1).start()

    for p in range(3):
        edges(p)
    for p in range(3):
        limit(p)

    table = rank_table(owner_ref, slot_ref, weight_ref)
    for p in range(3):
        states_copy(p, 1, 1).start()
        states_copy(p, 3, 0).start()
    for p in range(3):
        axes = PARTS[p][2]
        part_table(table, axes, tables[p])
        at[p][0] = tables[p][here[axes[0]]]
        for d in (2, 1, 3):
            table_copy(p, d).start()
    for p in range(3):
        for d in (1, 3):
            states_copy(p, d, d // 2).wait_recv()
            relay_copy(p, d).start()

    element = lax.broadcasted_iota(jnp.int32, (E, 256), 0).astype(F32)
    quarter = lax.rem(lax.broadcasted_iota(jnp.int32, (1, 256), 1) // CAP, 4)

    split = (sp0, sp1, sp2)

    def cut(p, d):
        first, count, _ = PARTS[p]
        rows = count * Q
        if d == 2:
            relay_copy(p, 1).wait_recv()
            relay_copy(p, 3).wait_recv()
        elif d:
            states_copy(p, d, 1 - d // 2).wait_recv()
        values = lim_ref[first * Q : first * Q + rows, :] if d == 0 else ar[p][3 - d]
        high, low = halves(values)
        split[p][(4 - d) % 4, 0:rows, :] = high
        split[p][(4 - d) % 4, rows : 2 * rows, :] = low

    def route(p, d):
        _, count, axes = PARTS[p]
        rows = count * Q
        group = lax.rem(here[axes[1]] + d, 4) * 2

        def info_of(j, what):
            tile = at[p][j, what]
            lanes = []
            for core in range(2):
                row = jnp.where(row8 == group + core, tile, 0.0)
                row = jnp.sum(row, axis=0, keepdims=True)
                lanes.append(pltpu.roll(row, CAP * j, 1) if j else row)
            return jnp.concatenate(lanes, axis=1)

        infos = []
        for j in range(4):
            infos.append([info_of(j, what) for what in (1, 2, 3)])
            hot = jnp.where(element == info_of(j, 0), 1.0, 0.0).astype(BF16)
            made = jnp.dot(split[p][j], hot, preferred_element_type=F32)
            picked[j, 0:rows, :] = made[0:rows] + made[rows:]
        slots = jnp.zeros((8, 256), F32)
        for o in range(4):
            which, slot, weight = infos[3]
            for j in range(3):
                mine = quarter == (o + j) % 4
                which = jnp.where(mine, infos[j][0], which)
                slot = jnp.where(mine, infos[j][1], slot)
                weight = jnp.where(mine, infos[j][2], weight)
            for f in range(count):
                part = slice(f * Q, (f + 1) * Q)
                values = picked[3, part, :]
                for j in range(3):
                    values = jnp.where(quarter == (o + j) % 4, picked[j, part, :], values)
                made = product(p_ref[...], values)
                chosen = made[3 * Q :]
                for k in range(3):
                    chosen = jnp.where(which == float(k), made[k * Q : (k + 1) * Q], chosen)
                chosen = chosen * weight
                place = slice(o * rows + f * Q, o * rows + (f + 1) * Q)
                bs[p][d, 0, place, :] = chosen[:, 0:128]
                bs[p][d, 1, place, :] = chosen[:, 128:256]
            slots = jnp.where(row256 == o, slot, slots)
        bs[p][d, 0, 4 * rows : 4 * rows + 8, :] = slots[:, 0:128]
        bs[p][d, 1, 4 * rows : 4 * rows + 8, :] = slots[:, 128:256]
        block_copy(p, d, 1).start()

        @pl.when(d > 0)
        def _():
            block_copy(p, d, 0).start()


    def gather(p, number):
        _, count, axes = PARTS[p]
        rows = count * Q
        me_c = here[axes[2]]
        d = (0, 1, 3, 2)[number]
        if d == 0:
            own_copy(p).wait()
        else:
            block_copy(p, d, 0).wait_recv()
        block_copy(p, d, 1).wait_recv()
        slot_of = (4 - d) % 4

        def owner(distance):
            o = lax.rem(me_c + distance, 4)
            place = pl.ds(pl.multiple_of(o * rows, rows), rows)
            high, low = halves(br[p][slot_of, place, :])
            pair[0:rows, :] = high
            pair[rows : 2 * rows, :] = low
            slot = br[p][slot_of, 4 * rows : 4 * rows + 8, :]
            slot = jnp.sum(jnp.where(row256 == o, slot, 0.0), axis=0, keepdims=True)
            hot = jnp.where(element == slot, 1.0, 0.0)
            made = lax.dot_general(
                pair[0 : 2 * rows, :],
                hot.astype(BF16),
                (((1,), (1,)), ((), ())),
                preferred_element_type=F32,
            )
            total = made[0:rows] + made[rows:]
            if number > 0:
                total = total + cs[p][o]
            cs[p][o] = total

        if number < 3:

            def step(distance, _):
                owner(distance)
                return 0

            lax.fori_loop(0, 4, step, 0)
        else:
            owner(2)
            far_sum(p, 1).start()
            far_sum(p, 3).start()
            owner(1)
            near_sum(p, 1, 1).start()
            owner(3)
            near_sum(p, 3, 0).start()
            owner(0)

    def combine(p):
        half = PARTS[p][1] * Q // 2
        for d in (1, 3):
            far_sum(p, d).wait_recv()
            o = owner_at(p, d)
            place = slice((d // 2) * half, (d // 2 + 1) * half)
            cs[p][o, place, :] = cs[p][o, place, :] + ct[p][d // 2]
            near_sum(p, d, d // 2).start()

    def finish(p):
        total = cs[p][here[PARTS[p][2][2]]]
        for d in (1, 3):
            for h in (0, 1):
                near_sum(p, d, h).wait_recv()
            total = total + cr[p][d // 2]
        out[p][...] = total

    for d in (0, 1, 3):
        for p in range(3):
            cut(p, d)
    for p in range(3):
        cut(p, 2)
        for d in (1, 2, 3):
            table_copy(p, d).wait_recv()

    def towards(step, _):
        d = lax.rem(6 - step + (step // 2) * (2 * step - 1), 4)
        for p in range(3):
            route(p, d)
        return 0

    lax.fori_loop(0, 4, towards, 0)
    for p in range(3):
        own_copy(p).start()
    for number in range(4):
        gather(2, number)
        if number == 0:
            gather(0, 0)
            gather(1, 0)
    combine(2)
    for number in range(1, 4):
        gather(0, number)
        gather(1, number)
    for p in (0, 1):
        combine(p)
    for p in (2, 0, 1):
        finish(p)
    for p in range(3):
        for s in range(4):
            side_copy(p, s).wait_send()
            mean_copy(p, s).wait_send()
        for d in (1, 3):
            for h in (0, 1):
                states_copy(p, d, h).wait_send()
                near_sum(p, d, h).wait_send()
            relay_copy(p, d).wait_send()
            far_sum(p, d).wait_send()
        for d in (1, 2, 3):
            table_copy(p, d).wait_send()
            block_copy(p, d, 0).wait_send()
            block_copy(p, d, 1).wait_send()
        block_copy(p, 0, 1).wait_send()


def body(
    states,
    swept_volume,
    flux_own,
    flux_next,
    mass_inverse,
    projection,
    new_owner,
    new_slot,
    intersection_weight,
):
    rows = [count * Q for _, count, _ in PARTS]
    dma = pltpu.SemaphoreType.DMA
    made = pl.pallas_call(
        kernel,
        out_shape=[jax.ShapeDtypeStruct((r, E), F32) for r in rows],
        in_specs=[pl.BlockSpec(memory_space=pl.ANY)] + [VMEM] * 5 + [HBM] * 3,
        out_specs=[VMEM] * 3,
        scratch_shapes=[
            pltpu.VMEM((K, E), jnp.int32),
            pltpu.VMEM((K, E), jnp.int32),
            pltpu.VMEM((K, E), F32),
            pltpu.VMEM((COLS, E), F32),
            pltpu.VMEM((8 * Q, 3 * Q), BF16),
            pltpu.VMEM((4 * Q, 3 * Q), BF16),
            pltpu.VMEM((COLS, E), F32),
            pltpu.VMEM((4, COLS, EY), F32),
            pltpu.VMEM((2, COLS, EY), F32),
            pltpu.VMEM((3, 8, E), F32),
            pltpu.VMEM((3, 4, 8, EY), F32),
            pltpu.VMEM((3, 2, 8, EY), F32),
        ]
        + [pltpu.VMEM((4, 4, 8, 128), F32) for r in rows]
        + [pltpu.VMEM((3, r, E), F32) for r in rows]
        + [pltpu.VMEM((4, 4, 8, 128), F32) for r in rows]
        + [pltpu.VMEM((4, 2, 4 * r + 8, 128), F32) for r in rows]
        + [pltpu.VMEM((4, 4 * r + 8, 256), F32) for r in rows]
        + [pltpu.VMEM((4, r, E), F32) for r in rows]
        + [pltpu.VMEM((2, r, E), F32) for r in rows]
        + [pltpu.VMEM((2, r // 2, E), F32) for r in rows]
        + [
            *[pltpu.VMEM((4, 2 * r, E), BF16) for r in rows],
            pltpu.VMEM((4, max(rows), 256), F32),
            pltpu.VMEM((2 * max(rows), 256), BF16),
            dma((EX + 3,)),
            *[dma((3, 4))] * 4,
            *[dma((3, 2, 2))] * 2,
            *[dma((3, 2))] * 2,
            *[dma((3, 3))] * 2,
            *[dma((3, 4, 2))] * 2,
            *[dma((3, 2, 2))] * 2,
            *[dma((3, 2))] * 2,
            dma((3,)),
        ],
        compiler_params=pltpu.CompilerParams(
            collective_id=0, has_side_effects=True, vmem_limit_bytes=56 * 2**20
        ),
    )(
        states.reshape(COLS, EX, EY),
        swept_volume,
        mass_inverse,
        flux_own,
        flux_next,
        projection,
        new_owner.reshape(E, K).T,
        new_slot.reshape(E, K).T,
        intersection_weight.reshape(E, K).T,
    )
    return jnp.concatenate(made, axis=0).reshape(F, Q, E)


def solution(mesh):
    placed = (
        P(None, None, "gx", "gy"),
        P(None, "gx", "gy"),
        P(),
        P(),
        P(),
        P(),
        P("gx", "gy", None, None),
        P("gx", "gy", None, None),
        P("gx", "gy", None, None),
    )
    return jax.shard_map(
        body, mesh=mesh, in_specs=placed, out_specs=P(None, None, ("gx", "gy")), check_vma=False
    )
```

```python
import functools

import jax
import jax.numpy as jnp
from jax import lax
from jax.experimental import pallas as pl
from jax.experimental.pallas import tpu as pltpu
from jax.sharding import PartitionSpec as P

F, Q, K, EX, EY, CAP = 8, 64, 4, 4, 128, 32
E = EX * EY
COLS = F * Q
MARGIN = 0.75
MESH = pl.DeviceIdType.MESH
VMEM = pl.BlockSpec(memory_space=pltpu.VMEM)
HBM = pl.BlockSpec(memory_space=pltpu.HBM)
F32, BF16 = jnp.float32, jnp.bfloat16
PARTS = ((0, 3, "xyz"), (3, 3, "yzx"), (6, 2, "zxy"))


def halves(values):
    high = values.astype(BF16)
    return high, (values - high.astype(F32)).astype(BF16)


def product(matrix, values):
    high, low = halves(values)
    stacked = jnp.concatenate([high, low, high], axis=0)
    return jnp.dot(matrix, stacked, preferred_element_type=F32)


def fold(inverse_ref, sources, target_ref):
    inverse = inverse_ref[...]
    for term, source in enumerate(sources):
        made = jnp.dot(
            inverse, source, precision=lax.Precision.HIGHEST, preferred_element_type=F32
        )
        high, low = halves(made)
        target_ref[term * Q : (term + 1) * Q, :] = jnp.concatenate([high, high, low], axis=1)


def rank_table(owner_ref, slot_ref, weight_ref):
    devices = lax.broadcasted_iota(jnp.int32, (128, 256), 0)
    ranks = lax.broadcasted_iota(jnp.int32, (CAP, 256), 0).astype(F32)
    earlier = lax.broadcasted_iota(jnp.int32, (256, 256), 0) < lax.broadcasted_iota(
        jnp.int32, (256, 256), 1
    )
    earlier = jnp.where(earlier, 1.0, 0.0).astype(BF16)
    carry = jnp.zeros((128, 1), F32)
    table = jnp.zeros((128, 8 * CAP), F32)
    for k in range(K):
        for start in range(0, E, 256):
            lanes = slice(start, start + 256)
            named = jnp.where(devices == owner_ref[k : k + 1, lanes], 1.0, 0.0)
            before = jnp.dot(named.astype(BF16), earlier, preferred_element_type=F32) + carry
            rank = jnp.sum(named * before, axis=0, keepdims=True)
            carry = carry + jnp.sum(named, axis=1, keepdims=True)
            placed = ranks == rank
            weight = weight_ref[k : k + 1, lanes]
            first = weight.astype(BF16).astype(F32)
            second = (weight - first).astype(BF16).astype(F32)
            slot = slot_ref[k : k + 1, lanes]
            element = lax.broadcasted_iota(jnp.int32, (1, 256), 1) + (start + 1)
            parts = [
                (element // 128).astype(F32),
                lax.rem(element, 128).astype(F32),
                jnp.full((1, 256), float(k), F32),
                (slot // 128).astype(F32),
                lax.rem(slot, 128).astype(F32),
                first,
                second,
                weight - first - second,
            ]
            values = jnp.concatenate([jnp.where(placed, row, 0.0) for row in parts], axis=0)
            table = table + lax.dot_general(
                named.astype(BF16),
                values.astype(BF16),
                (((1,), (1,)), ((), ())),
                preferred_element_type=F32,
            )
    return table.astype(BF16)


STRIDE = {"z": 32, "y": 8, "x": 2}


def part_table(table, axes, target_ref):
    a, b, c = axes
    row = lax.broadcasted_iota(jnp.int32, (32, 128), 0)
    lane = lax.broadcasted_iota(jnp.int32, (32, 128), 1)
    first = (row // 8) * STRIDE[a] + lax.rem(row // 2, 4) * STRIDE[b] + lax.rem(row, 2)
    quarter = lane // CAP
    made = [jnp.zeros((32, 128), F32)] * 8
    for o in range(4):
        chosen = jnp.where(lane == first + o * STRIDE[c], 1.0, 0.0).astype(BF16)
        found = jnp.dot(chosen, table, preferred_element_type=F32)
        for m in range(8):
            tile = found[:, (m // 4) * 128 : (m // 4 + 1) * 128]
            turn = (o - m % 4) % 4
            tile = pltpu.roll(tile, turn * CAP, 1) if turn else tile
            made[m] = jnp.where(quarter == o, tile, made[m])
    whats = (
        made[0] * 128 + made[1] - 1,
        made[2],
        made[3] * 128 + made[4],
        made[5] + made[6] + made[7],
    )
    for place in range(4):
        for number, what in enumerate(whats):
            target_ref[place, number] = what[place * 8 : (place + 1) * 8]


def kernel(
    states_ref, v_ref, inverse_ref, own_ref, next_ref, project_ref,
    owner_hbm, slot_hbm, weight_hbm, out0, out1, out2, owner_ref, slot_ref, weight_ref, u_ref, g_ref, p_ref, lim_ref, sides, packed, means, mean_sides, mean_packed,
    tb0, tb1, tb2, ar0, ar1, ar2, at0, at1, at2, bs0, bs1, bs2, br0, br1, br2,
    cs0, cs1, cs2, cr0, cr1, cr2, ct0, ct1, ct2, sp0, sp1, sp2, picked, pair,
    u_sem, h_send, h_recv, m_send, m_recv,
    a_send, a_recv, f_send, f_recv, t_send, t_recv, b_send, b_recv, c_send, c_recv, d_send, d_recv,
    own_sem,
):
    tables, ar, at = (tb0, tb1, tb2), (ar0, ar1, ar2), (at0, at1, at2)
    bs, br, cs, cr = (bs0, bs1, bs2), (br0, br1, br2), (cs0, cs1, cs2), (cr0, cr1, cr2)
    ct, out = (ct0, ct1, ct2), (out0, out1, out2)
    gx, gy = lax.axis_index("gx"), lax.axis_index("gy")
    n_x, n_y = lax.axis_size("gx"), lax.axis_size("gy")
    here = {"x": gy // 2, "y": lax.rem(gx, 4), "z": gx // 4, "c": lax.rem(gy, 2)}
    near = (
        (lax.rem(gx + n_x - 1, n_x), gy),
        (lax.rem(gx + 1, n_x), gy),
        (gx, lax.rem(gy + n_y - 1, n_y)),
        (gx, lax.rem(gy + 1, n_y)),
    )
    inside = (gx > 0, gx < n_x - 1, gy > 0, gy < n_y - 1)
    gate = [jnp.where(there, 1.0, 0.0).astype(F32) for there in inside]

    def away(axis, distance, core=0):
        at_ = dict(here)
        at_[axis] = lax.rem(here[axis] + distance, 4)
        at_["c"] = lax.rem(here["c"] + core, 2)
        return (at_["z"] * 4 + at_["y"], at_["x"] * 2 + at_["c"])

    partners = [away(axis, d, core) for axis in "xyz" for d in (1, 2, 3) for core in (0, 1)]
    partners += [away("x", 0, 1), *near[:2]]
    loads = [
        pltpu.make_async_copy(
            states_ref.at[:, j, :], u_ref.at[:, pl.ds(j * EY, EY)], u_sem.at[j]
        )
        for j in range(EX)
    ]
    lists = [
        pltpu.make_async_copy(source, target, u_sem.at[EX + i])
        for i, (source, target) in enumerate(
            ((owner_hbm, owner_ref), (slot_hbm, slot_ref), (weight_hbm, weight_ref))
        )
    ]
    for load in loads + lists:
        load.start()
    barrier = pltpu.get_barrier_semaphore()
    for device in partners:
        pl.semaphore_signal(barrier, inc=1, device_id=device, device_id_type=MESH)

    def remote(source, target, send, recv, device):
        return pltpu.make_async_remote_copy(
            src_ref=source,
            dst_ref=target,
            send_sem=send,
            recv_sem=recv,
            device_id=device,
            device_id_type=MESH,
        )

    def rows_of(p):
        first, count, _ = PARTS[p]
        return pl.ds(first * Q, count * Q)

    def side_copy(p, s):
        rows = rows_of(p)
        source = (
            u_ref.at[rows, pl.ds(0, EY)],
            u_ref.at[rows, pl.ds(3 * EY, EY)],
            packed.at[0, rows],
            packed.at[1, rows],
        )[s]
        return remote(
            source, sides.at[s ^ 1, rows], h_send.at[p, s], h_recv.at[p, s ^ 1], near[s]
        )

    def mean_copy(p, s):
        source = (
            means.at[p, :, pl.ds(0, EY)],
            means.at[p, :, pl.ds(3 * EY, EY)],
            mean_packed.at[p, 0],
            mean_packed.at[p, 1],
        )[s]
        return remote(
            source, mean_sides.at[p, s ^ 1], m_send.at[p, s], m_recv.at[p, s ^ 1], near[s]
        )

    def half_of(p, h):
        size = PARTS[p][1] * Q // 2
        return pl.ds(h * size, size)

    def states_copy(p, d, h):
        first, count, axes = PARTS[p]
        size = count * Q // 2
        return remote(
            lim_ref.at[pl.ds(first * Q + h * size, size)],
            ar[p].at[3 - d, half_of(p, h)],
            a_send.at[p, d // 2, h],
            a_recv.at[p, d // 2, h],
            away(axes[0], d),
        )

    def relay_copy(p, d):
        half = half_of(p, d // 2)
        return remote(
            ar[p].at[3 - d, half],
            ar[p].at[1, half],
            f_send.at[p, d // 2],
            f_recv.at[p, d // 2],
            away(PARTS[p][2][0], d),
        )

    def table_copy(p, d):
        axis = PARTS[p][2][0]
        return remote(
            tables[p].at[lax.rem(here[axis] + d, 4)],
            at[p].at[4 - d],
            t_send.at[p, d - 1],
            t_recv.at[p, d - 1],
            away(axis, d),
        )

    def block_copy(p, d, core):
        return remote(
            bs[p].at[d, lax.rem(here["c"] + core, 2)],
            br[p].at[lax.rem(4 - d, 4), :, pl.ds(core * 128, 128)],
            b_send.at[p, d, core],
            b_recv.at[p, d, core],
            away(PARTS[p][2][1], d, core),
        )

    def own_copy(p):
        return pltpu.make_async_copy(
            bs[p].at[0, here["c"]], br[p].at[0, :, pl.ds(0, 128)], own_sem.at[p]
        )

    def owner_at(p, d):
        return lax.rem(here[PARTS[p][2][2]] + d, 4)

    def far_sum(p, d):
        return remote(
            cs[p].at[owner_at(p, 2), half_of(p, d // 2)],
            ct[p].at[d // 2],
            d_send.at[p, d // 2],
            d_recv.at[p, d // 2],
            away(PARTS[p][2][2], d),
        )

    def near_sum(p, d, h):
        half = half_of(p, h)
        return remote(
            cs[p].at[owner_at(p, d), half],
            cr[p].at[d // 2, half],
            c_send.at[p, d // 2, h],
            c_recv.at[p, d // 2, h],
            away(PARTS[p][2][2], d),
        )

    lane64 = lax.broadcasted_iota(jnp.int32, (Q, EY), 1)
    lane8 = lax.broadcasted_iota(jnp.int32, (8, EY), 1)
    row8 = lax.broadcasted_iota(jnp.int32, (8, EY), 0)
    row256 = lax.broadcasted_iota(jnp.int32, (8, 256), 0)

    def block(j):
        return slice(j * EY, (j + 1) * EY)

    def pack(f, _):
        rows = pl.ds(pl.multiple_of(f * Q, Q), Q)
        low = jnp.zeros((Q, EY), F32)
        high = jnp.zeros((Q, EY), F32)
        for j in range(EX):
            values = u_ref[rows, block(j)]
            low = jnp.where(lane64 == j, pltpu.roll(values, j, 1) if j else values, low)
            high = jnp.where(lane64 == j, pltpu.roll(values, j + 1, 1), high)
        packed[0, rows, :] = low
        packed[1, rows, :] = high
        return 0

    for load in loads + lists:
        load.wait()
    lax.fori_loop(0, F, pack, 0)
    fold(inverse_ref, [own_ref[s] for s in range(4)] + [next_ref[s] for s in range(4)], g_ref)
    fold(inverse_ref, [project_ref[k] for k in range(4)], p_ref)
    pl.semaphore_wait(barrier, len(partners))
    for p in range(3):
        for s in range(4):
            side_copy(p, s).start()

    def interior(f, _):
        rows = pl.ds(pl.multiple_of(f * Q, Q), Q)
        u = u_ref[rows, :]
        made = product(g_ref[...], u)
        for j in range(EX):
            total = u[:, block(j)]
            for s in range(4):
                outward = jnp.maximum(v_ref[s, j : j + 1, :], 0.0)
                total = total - outward * made[s * Q : (s + 1) * Q, block(j)]
            inward = [jnp.minimum(v_ref[s, j : j + 1, :], 0.0) for s in range(4)]
            if j > 0:
                total = total - inward[0] * made[4 * Q : 5 * Q, block(j - 1)]
            if j < EX - 1:
                total = total - inward[1] * made[5 * Q : 6 * Q, block(j + 1)]
            before = pltpu.roll(made[6 * Q : 7 * Q, block(j)], 1, 1)
            after = pltpu.roll(made[7 * Q : 8 * Q, block(j)], EY - 1, 1)
            total = total - jnp.where(lane64 == 0, 0.0, inward[2] * before)
            total = total - jnp.where(lane64 == EY - 1, 0.0, inward[3] * after)
            lim_ref[rows, block(j)] = total
        return 0

    lax.fori_loop(0, F, interior, 0)

    def edges(p):
        first, count, _ = PARTS[p]
        for s in range(4):
            side_copy(p, s).wait_recv()

        def field(f, found):
            found = list(found)
            rows = pl.ds(pl.multiple_of((first + f) * Q, Q), Q)
            made = [
                product(g_ref[(4 + s) * Q : (5 + s) * Q, :], sides[s, rows, :]) for s in range(4)
            ]
            for j in range(EX):
                inward = [jnp.minimum(v_ref[s, j : j + 1, :], 0.0) * gate[s] for s in range(4)]
                total = lim_ref[rows, block(j)]
                if j == 0:
                    total = total - inward[0] * made[0]
                if j == EX - 1:
                    total = total - inward[1] * made[1]
                before = made[2] if j == 0 else pltpu.roll(made[2], EY - j, 1)
                after = pltpu.roll(made[3], EY - 1 - j, 1)
                total = total - jnp.where(lane64 == 0, inward[2] * before, 0.0)
                total = total - jnp.where(lane64 == EY - 1, inward[3] * after, 0.0)
                lim_ref[rows, block(j)] = total
                mean = jnp.sum(total, axis=0, keepdims=True) * (1.0 / Q)
                found[j] = jnp.where(row8 == f, mean, found[j])
            return tuple(found)

        found = lax.fori_loop(
            0, count, field, tuple(jnp.zeros((8, EY), F32) for _ in range(EX))
        )
        low = jnp.zeros((8, EY), F32)
        high = jnp.zeros((8, EY), F32)
        for j in range(EX):
            means[p, :, block(j)] = found[j]
            low = jnp.where(lane8 == j, pltpu.roll(found[j], j, 1) if j else found[j], low)
            high = jnp.where(lane8 == j, pltpu.roll(found[j], j + 1, 1), high)
        mean_packed[p, 0] = low
        mean_packed[p, 1] = high
        for s in range(4):
            mean_copy(p, s).start()

    def limit(p):
        first, count, _ = PARTS[p]
        for s in range(4):
            mean_copy(p, s).wait_recv()
        for j in range(EX):
            center = means[p, :, block(j)]
            if j > 0:
                left = means[p, :, block(j - 1)]
            else:
                left = jnp.where(gate[0] > 0, mean_sides[p, 0], center)
            if j < EX - 1:
                right = means[p, :, block(j + 1)]
            else:
                right = jnp.where(gate[1] > 0, mean_sides[p, 1], center)
            before = mean_sides[p, 2] if j == 0 else pltpu.roll(mean_sides[p, 2], EY - j, 1)
            before = jnp.where(gate[2] > 0, before, center)
            before = jnp.where(lane8 == 0, before, pltpu.roll(center, 1, 1))
            after = pltpu.roll(mean_sides[p, 3], EY - 1 - j, 1)
            after = jnp.where(gate[3] > 0, after, center)
            after = jnp.where(lane8 == EY - 1, after, pltpu.roll(center, EY - 1, 1))
            lower, upper = center, center
            for other in (left, right, before, after):
                lower = jnp.minimum(lower, other)
                upper = jnp.maximum(upper, other)
            lower, upper = lower - MARGIN, upper + MARGIN
            for f in range(count):
                rows = slice((first + f) * Q, (first + f + 1) * Q)
                values = jnp.maximum(lim_ref[rows, block(j)], lower[f : f + 1])
                lim_ref[rows, block(j)] = jnp.minimum(values, upper[f : f + 1])
        states_copy(p, 1, 0).start()
        states_copy(p, 3, 1).start()

    for p in range(3):
        edges(p)
    for p in range(3):
        limit(p)

    table = rank_table(owner_ref, slot_ref, weight_ref)
    for p in range(3):
        states_copy(p, 1, 1).start()
        states_copy(p, 3, 0).start()
    for p in range(3):
        axes = PARTS[p][2]
        part_table(table, axes, tables[p])
        at[p][0] = tables[p][here[axes[0]]]
        for d in (2, 1, 3):
            table_copy(p, d).start()
    for p in range(3):
        for d in (1, 3):
            states_copy(p, d, d // 2).wait_recv()
            relay_copy(p, d).start()

    element = lax.broadcasted_iota(jnp.int32, (E, 256), 0).astype(F32)
    quarter = lax.rem(lax.broadcasted_iota(jnp.int32, (1, 256), 1) // CAP, 4)

    split = (sp0, sp1, sp2)

    def cut(p, d):
        first, count, _ = PARTS[p]
        rows = count * Q
        if d == 2:
            relay_copy(p, 1).wait_recv()
            relay_copy(p, 3).wait_recv()
        elif d:
            states_copy(p, d, 1 - d // 2).wait_recv()
        values = lim_ref[first * Q : first * Q + rows, :] if d == 0 else ar[p][3 - d]
        high, low = halves(values)
        split[p][(4 - d) % 4, 0:rows, :] = high
        split[p][(4 - d) % 4, rows : 2 * rows, :] = low

    def route(p, d):
        _, count, axes = PARTS[p]
        rows = count * Q
        group = lax.rem(here[axes[1]] + d, 4) * 2

        def info_of(j, what):
            tile = at[p][j, what]
            lanes = []
            for core in range(2):
                row = jnp.where(row8 == group + core, tile, 0.0)
                row = jnp.sum(row, axis=0, keepdims=True)
                lanes.append(pltpu.roll(row, CAP * j, 1) if j else row)
            return jnp.concatenate(lanes, axis=1)

        infos = []
        for j in range(4):
            infos.append([info_of(j, what) for what in (1, 2, 3)])
            hot = jnp.where(element == info_of(j, 0), 1.0, 0.0).astype(BF16)
            made = jnp.dot(split[p][j], hot, preferred_element_type=F32)
            picked[j, 0:rows, :] = made[0:rows] + made[rows:]
        slots = jnp.zeros((8, 256), F32)
        for o in range(4):
            which, slot, weight = infos[3]
            for j in range(3):
                mine = quarter == (o + j) % 4
                which = jnp.where(mine, infos[j][0], which)
                slot = jnp.where(mine, infos[j][1], slot)
                weight = jnp.where(mine, infos[j][2], weight)
            for f in range(count):
                part = slice(f * Q, (f + 1) * Q)
                values = picked[3, part, :]
                for j in range(3):
                    values = jnp.where(quarter == (o + j) % 4, picked[j, part, :], values)
                made = product(p_ref[...], values)
                chosen = made[3 * Q :]
                for k in range(3):
                    chosen = jnp.where(which == float(k), made[k * Q : (k + 1) * Q], chosen)
                chosen = chosen * weight
                place = slice(o * rows + f * Q, o * rows + (f + 1) * Q)
                bs[p][d, 0, place, :] = chosen[:, 0:128]
                bs[p][d, 1, place, :] = chosen[:, 128:256]
            slots = jnp.where(row256 == o, slot, slots)
        bs[p][d, 0, 4 * rows : 4 * rows + 8, :] = slots[:, 0:128]
        bs[p][d, 1, 4 * rows : 4 * rows + 8, :] = slots[:, 128:256]
        block_copy(p, d, 1).start()

        @pl.when(d > 0)
        def _():
            block_copy(p, d, 0).start()


    def landed(p, number):
        d = (0, 1, 3, 2)[number]
        if d == 0:
            own_copy(p).wait()
        else:
            block_copy(p, d, 0).wait_recv()
        block_copy(p, d, 1).wait_recv()

    def arrived(p, number, distance):
        _, count, axes = PARTS[p]
        rows = count * Q
        slot_of = (0, 3, 1, 2)[number]
        o = lax.rem(here[axes[2]] + distance, 4)
        place = pl.ds(pl.multiple_of(o * rows, rows), rows)
        high, low = halves(br[p][slot_of, place, :])
        pair[0:rows, :] = high
        pair[rows : 2 * rows, :] = low
        slot = br[p][slot_of, 4 * rows : 4 * rows + 8, :]
        slot = jnp.sum(jnp.where(row256 == o, slot, 0.0), axis=0, keepdims=True)
        hot = jnp.where(element == slot, 1.0, 0.0)
        made = lax.dot_general(
            pair[0 : 2 * rows, :],
            hot.astype(BF16),
            (((1,), (1,)), ((), ())),
            preferred_element_type=F32,
        )
        total = made[0:rows] + made[rows:]
        if number > 0:
            total = total + cs[p][o]
        cs[p][o] = total

    def gather(p, number):
        landed(p, number)

        def step(distance, _):
            arrived(p, number, distance)
            return 0

        lax.fori_loop(0, 4, step, 0)

    def gather_last(ps):
        for distance in (2, 1, 3, 0):
            for p in ps:
                if distance == 2:
                    landed(p, 3)
                arrived(p, 3, distance)
                if distance == 2:
                    far_sum(p, 1).start()
                    far_sum(p, 3).start()
        for p in ps:
            near_sum(p, 1, 1).start()
            near_sum(p, 3, 0).start()

    def combine(p):
        half = PARTS[p][1] * Q // 2
        for d in (1, 3):
            far_sum(p, d).wait_recv()
            o = owner_at(p, d)
            place = slice((d // 2) * half, (d // 2 + 1) * half)
            cs[p][o, place, :] = cs[p][o, place, :] + ct[p][d // 2]
            near_sum(p, d, d // 2).start()

    def finish(p):
        for h in (0, 1):
            near_sum(p, 1, h).wait_recv()
            near_sum(p, 3, h).wait_recv()
        out[p][...] = cs[p][owner_at(p, 0)] + cr[p][0] + cr[p][1]

    for d in (0, 1, 3):
        for p in range(3):
            cut(p, d)
    for p in range(3):
        cut(p, 2)
        for d in (1, 2, 3):
            table_copy(p, d).wait_recv()

    def towards(step, _):
        d = lax.rem(6 - step + (step // 2) * (2 * step - 1), 4)
        for p in range(3):
            route(p, d)
        return 0

    lax.fori_loop(0, 4, towards, 0)
    for p in range(3):
        own_copy(p).start()
    for p in (2, 0, 1):
        gather(p, 0)
    gather(2, 1)
    gather(2, 2)
    for number in (1, 2):
        gather(0, number)
        gather(1, number)
    gather_last((0, 1, 2))
    for p in (0, 1, 2):
        combine(p)
    for p in (0, 1, 2):
        finish(p)
    for p in range(3):
        for s in range(4):
            side_copy(p, s).wait_send()
            mean_copy(p, s).wait_send()
        for d in (1, 3):
            for h in (0, 1):
                states_copy(p, d, h).wait_send()
                near_sum(p, d, h).wait_send()
            relay_copy(p, d).wait_send()
            far_sum(p, d).wait_send()
        for d in (1, 2, 3):
            table_copy(p, d).wait_send()
            block_copy(p, d, 0).wait_send()
            block_copy(p, d, 1).wait_send()
        block_copy(p, 0, 1).wait_send()


def body(
    states,
    swept_volume,
    flux_own,
    flux_next,
    mass_inverse,
    projection,
    new_owner,
    new_slot,
    intersection_weight,
):
    rows = [count * Q for _, count, _ in PARTS]
    dma = pltpu.SemaphoreType.DMA
    made = pl.pallas_call(
        kernel,
        out_shape=[jax.ShapeDtypeStruct((r, E), F32) for r in rows],
        in_specs=[pl.BlockSpec(memory_space=pl.ANY)] + [VMEM] * 5 + [HBM] * 3,
        out_specs=[VMEM] * 3,
        scratch_shapes=[
            pltpu.VMEM((K, E), jnp.int32),
            pltpu.VMEM((K, E), jnp.int32),
            pltpu.VMEM((K, E), F32),
            pltpu.VMEM((COLS, E), F32),
            pltpu.VMEM((8 * Q, 3 * Q), BF16),
            pltpu.VMEM((4 * Q, 3 * Q), BF16),
            pltpu.VMEM((COLS, E), F32),
            pltpu.VMEM((4, COLS, EY), F32),
            pltpu.VMEM((2, COLS, EY), F32),
            pltpu.VMEM((3, 8, E), F32),
            pltpu.VMEM((3, 4, 8, EY), F32),
            pltpu.VMEM((3, 2, 8, EY), F32),
        ]
        + [pltpu.VMEM((4, 4, 8, 128), F32) for r in rows]
        + [pltpu.VMEM((3, r, E), F32) for r in rows]
        + [pltpu.VMEM((4, 4, 8, 128), F32) for r in rows]
        + [pltpu.VMEM((4, 2, 4 * r + 8, 128), F32) for r in rows]
        + [pltpu.VMEM((4, 4 * r + 8, 256), F32) for r in rows]
        + [pltpu.VMEM((4, r, E), F32) for r in rows]
        + [pltpu.VMEM((2, r, E), F32) for r in rows]
        + [pltpu.VMEM((2, r // 2, E), F32) for r in rows]
        + [
            *[pltpu.VMEM((4, 2 * r, E), BF16) for r in rows],
            pltpu.VMEM((4, max(rows), 256), F32),
            pltpu.VMEM((2 * max(rows), 256), BF16),
            dma((EX + 3,)),
            *[dma((3, 4))] * 4,
            *[dma((3, 2, 2))] * 2,
            *[dma((3, 2))] * 2,
            *[dma((3, 3))] * 2,
            *[dma((3, 4, 2))] * 2,
            *[dma((3, 2, 2))] * 2,
            *[dma((3, 2))] * 2,
            dma((3,)),
        ],
        compiler_params=pltpu.CompilerParams(
            collective_id=0, has_side_effects=True, vmem_limit_bytes=56 * 2**20
        ),
    )(
        states.reshape(COLS, EX, EY),
        swept_volume,
        mass_inverse,
        flux_own,
        flux_next,
        projection,
        new_owner.reshape(E, K).T,
        new_slot.reshape(E, K).T,
        intersection_weight.reshape(E, K).T,
    )
    return jnp.concatenate(made, axis=0).reshape(F, Q, E)


def solution(mesh):
    placed = (
        P(None, None, "gx", "gy"),
        P(None, "gx", "gy"),
        P(),
        P(),
        P(),
        P(),
        P("gx", "gy", None, None),
        P("gx", "gy", None, None),
        P("gx", "gy", None, None),
    )
    return jax.shard_map(
        body, mesh=mesh, in_specs=placed, out_specs=P(None, None, ("gx", "gy")), check_vma=False
    )
```

```python
import functools

import jax
import jax.numpy as jnp
from jax import lax
from jax.experimental import pallas as pl
from jax.experimental.pallas import tpu as pltpu
from jax.sharding import PartitionSpec as P

F, Q, K, EX, EY, CAP = 8, 64, 4, 4, 128, 32
E = EX * EY
COLS = F * Q
MARGIN = 0.75
MESH = pl.DeviceIdType.MESH
VMEM = pl.BlockSpec(memory_space=pltpu.VMEM)
HBM = pl.BlockSpec(memory_space=pltpu.HBM)
F32, BF16 = jnp.float32, jnp.bfloat16
PARTS = ((0, 3, "xyz"), (3, 3, "yzx"), (6, 2, "zxy"))


def halves(values):
    high = values.astype(BF16)
    return high, (values - high.astype(F32)).astype(BF16)


def product(matrix, values):
    high, low = halves(values)
    stacked = jnp.concatenate([high, low, high], axis=0)
    return jnp.dot(matrix, stacked, preferred_element_type=F32)


def fold(inverse_ref, sources, target_ref):
    inverse = inverse_ref[...]
    for term, source in enumerate(sources):
        made = jnp.dot(
            inverse, source, precision=lax.Precision.HIGHEST, preferred_element_type=F32
        )
        high, low = halves(made)
        target_ref[term * Q : (term + 1) * Q, :] = jnp.concatenate([high, high, low], axis=1)


def rank_table(owner_ref, slot_ref, weight_ref):
    devices = lax.broadcasted_iota(jnp.int32, (128, 256), 0)
    ranks = lax.broadcasted_iota(jnp.int32, (CAP, 256), 0).astype(F32)
    earlier = lax.broadcasted_iota(jnp.int32, (256, 256), 0) < lax.broadcasted_iota(
        jnp.int32, (256, 256), 1
    )
    earlier = jnp.where(earlier, 1.0, 0.0).astype(BF16)
    carry = jnp.zeros((128, 1), F32)
    table = jnp.zeros((128, 8 * CAP), F32)
    for k in range(K):
        for start in range(0, E, 256):
            lanes = slice(start, start + 256)
            named = jnp.where(devices == owner_ref[k : k + 1, lanes], 1.0, 0.0)
            before = jnp.dot(named.astype(BF16), earlier, preferred_element_type=F32) + carry
            rank = jnp.sum(named * before, axis=0, keepdims=True)
            carry = carry + jnp.sum(named, axis=1, keepdims=True)
            placed = ranks == rank
            weight = weight_ref[k : k + 1, lanes]
            first = weight.astype(BF16).astype(F32)
            second = (weight - first).astype(BF16).astype(F32)
            slot = slot_ref[k : k + 1, lanes]
            element = lax.broadcasted_iota(jnp.int32, (1, 256), 1) + (start + 1)
            parts = [
                (element // 128).astype(F32),
                lax.rem(element, 128).astype(F32),
                jnp.full((1, 256), float(k), F32),
                (slot // 128).astype(F32),
                lax.rem(slot, 128).astype(F32),
                first,
                second,
                weight - first - second,
            ]
            values = jnp.concatenate([jnp.where(placed, row, 0.0) for row in parts], axis=0)
            table = table + lax.dot_general(
                named.astype(BF16),
                values.astype(BF16),
                (((1,), (1,)), ((), ())),
                preferred_element_type=F32,
            )
    return table.astype(BF16)


STRIDE = {"z": 32, "y": 8, "x": 2}


def part_table(table, axes, target_ref):
    a, b, c = axes
    row = lax.broadcasted_iota(jnp.int32, (32, 128), 0)
    lane = lax.broadcasted_iota(jnp.int32, (32, 128), 1)
    first = (row // 8) * STRIDE[a] + lax.rem(row // 2, 4) * STRIDE[b] + lax.rem(row, 2)
    quarter = lane // CAP
    made = [jnp.zeros((32, 128), F32)] * 8
    for o in range(4):
        chosen = jnp.where(lane == first + o * STRIDE[c], 1.0, 0.0).astype(BF16)
        found = jnp.dot(chosen, table, preferred_element_type=F32)
        for m in range(8):
            tile = found[:, (m // 4) * 128 : (m // 4 + 1) * 128]
            turn = (o - m % 4) % 4
            tile = pltpu.roll(tile, turn * CAP, 1) if turn else tile
            made[m] = jnp.where(quarter == o, tile, made[m])
    whats = (
        made[0] * 128 + made[1] - 1,
        made[2],
        made[3] * 128 + made[4],
        made[5] + made[6] + made[7],
    )
    for place in range(4):
        for number, what in enumerate(whats):
            target_ref[place, number] = what[place * 8 : (place + 1) * 8]


def kernel(
    states_ref, v_ref, inverse_ref, own_ref, next_ref, project_ref,
    owner_hbm, slot_hbm, weight_hbm, out0, out1, out2, owner_ref, slot_ref, weight_ref, u_ref, g_ref, p_ref, lim_ref, sides, packed, means, mean_sides, mean_packed,
    tb0, tb1, tb2, ar0, ar1, ar2, at0, at1, at2, bs0, bs1, bs2, br0, br1, br2,
    cs0, cs1, cs2, cr0, cr1, cr2, ct0, ct1, ct2, sp0, sp1, sp2, pk0, pk1, pk2, pair,
    u_sem, h_send, h_recv, m_send, m_recv,
    a_send, a_recv, f_send, f_recv, t_send, t_recv, b_send, b_recv, c_send, c_recv, d_send, d_recv,
    own_sem,
):
    tables, ar, at = (tb0, tb1, tb2), (ar0, ar1, ar2), (at0, at1, at2)
    bs, br, cs, cr = (bs0, bs1, bs2), (br0, br1, br2), (cs0, cs1, cs2), (cr0, cr1, cr2)
    ct, out = (ct0, ct1, ct2), (out0, out1, out2)
    gx, gy = lax.axis_index("gx"), lax.axis_index("gy")
    n_x, n_y = lax.axis_size("gx"), lax.axis_size("gy")
    here = {"x": gy // 2, "y": lax.rem(gx, 4), "z": gx // 4, "c": lax.rem(gy, 2)}
    near = (
        (lax.rem(gx + n_x - 1, n_x), gy),
        (lax.rem(gx + 1, n_x), gy),
        (gx, lax.rem(gy + n_y - 1, n_y)),
        (gx, lax.rem(gy + 1, n_y)),
    )
    inside = (gx > 0, gx < n_x - 1, gy > 0, gy < n_y - 1)
    gate = [jnp.where(there, 1.0, 0.0).astype(F32) for there in inside]

    def away(axis, distance, core=0):
        at_ = dict(here)
        at_[axis] = lax.rem(here[axis] + distance, 4)
        at_["c"] = lax.rem(here["c"] + core, 2)
        return (at_["z"] * 4 + at_["y"], at_["x"] * 2 + at_["c"])

    partners = [away(axis, d, core) for axis in "xyz" for d in (1, 2, 3) for core in (0, 1)]
    partners += [away("x", 0, 1), *near[:2]]
    loads = [
        pltpu.make_async_copy(
            states_ref.at[:, j, :], u_ref.at[:, pl.ds(j * EY, EY)], u_sem.at[j]
        )
        for j in range(EX)
    ]
    lists = [
        pltpu.make_async_copy(source, target, u_sem.at[EX + i])
        for i, (source, target) in enumerate(
            ((owner_hbm, owner_ref), (slot_hbm, slot_ref), (weight_hbm, weight_ref))
        )
    ]
    for load in loads + lists:
        load.start()
    barrier = pltpu.get_barrier_semaphore()
    for device in partners:
        pl.semaphore_signal(barrier, inc=1, device_id=device, device_id_type=MESH)

    def remote(source, target, send, recv, device):
        return pltpu.make_async_remote_copy(
            src_ref=source,
            dst_ref=target,
            send_sem=send,
            recv_sem=recv,
            device_id=device,
            device_id_type=MESH,
        )

    def rows_of(p):
        first, count, _ = PARTS[p]
        return pl.ds(first * Q, count * Q)

    def side_copy(p, s):
        rows = rows_of(p)
        source = (
            u_ref.at[rows, pl.ds(0, EY)],
            u_ref.at[rows, pl.ds(3 * EY, EY)],
            packed.at[0, rows],
            packed.at[1, rows],
        )[s]
        return remote(
            source, sides.at[s ^ 1, rows], h_send.at[p, s], h_recv.at[p, s ^ 1], near[s]
        )

    def mean_copy(p, s):
        source = (
            means.at[p, :, pl.ds(0, EY)],
            means.at[p, :, pl.ds(3 * EY, EY)],
            mean_packed.at[p, 0],
            mean_packed.at[p, 1],
        )[s]
        return remote(
            source, mean_sides.at[p, s ^ 1], m_send.at[p, s], m_recv.at[p, s ^ 1], near[s]
        )

    def half_of(p, h):
        size = PARTS[p][1] * Q // 2
        return pl.ds(h * size, size)

    def states_copy(p, d, h):
        first, count, axes = PARTS[p]
        size = count * Q // 2
        return remote(
            lim_ref.at[pl.ds(first * Q + h * size, size)],
            ar[p].at[3 - d, half_of(p, h)],
            a_send.at[p, d // 2, h],
            a_recv.at[p, d // 2, h],
            away(axes[0], d),
        )

    def relay_copy(p, d):
        half = half_of(p, d // 2)
        return remote(
            ar[p].at[3 - d, half],
            ar[p].at[1, half],
            f_send.at[p, d // 2],
            f_recv.at[p, d // 2],
            away(PARTS[p][2][0], d),
        )

    def table_copy(p, d):
        axis = PARTS[p][2][0]
        return remote(
            tables[p].at[lax.rem(here[axis] + d, 4)],
            at[p].at[4 - d],
            t_send.at[p, d - 1],
            t_recv.at[p, d - 1],
            away(axis, d),
        )

    def block_copy(p, d, core):
        return remote(
            bs[p].at[d, lax.rem(here["c"] + core, 2)],
            br[p].at[lax.rem(4 - d, 4), :, pl.ds(core * 128, 128)],
            b_send.at[p, d, core],
            b_recv.at[p, d, core],
            away(PARTS[p][2][1], d, core),
        )

    def own_copy(p):
        return pltpu.make_async_copy(
            bs[p].at[0, here["c"]], br[p].at[0, :, pl.ds(0, 128)], own_sem.at[p]
        )

    def owner_at(p, d):
        return lax.rem(here[PARTS[p][2][2]] + d, 4)

    def far_sum(p, d):
        return remote(
            cs[p].at[owner_at(p, 2), half_of(p, d // 2)],
            ct[p].at[d // 2],
            d_send.at[p, d // 2],
            d_recv.at[p, d // 2],
            away(PARTS[p][2][2], d),
        )

    def near_sum(p, d, h):
        half = half_of(p, h)
        return remote(
            cs[p].at[owner_at(p, d), half],
            cr[p].at[d // 2, half],
            c_send.at[p, d // 2, h],
            c_recv.at[p, d // 2, h],
            away(PARTS[p][2][2], d),
        )

    lane64 = lax.broadcasted_iota(jnp.int32, (Q, EY), 1)
    lane8 = lax.broadcasted_iota(jnp.int32, (8, EY), 1)
    row8 = lax.broadcasted_iota(jnp.int32, (8, EY), 0)
    row256 = lax.broadcasted_iota(jnp.int32, (8, 256), 0)

    def block(j):
        return slice(j * EY, (j + 1) * EY)

    def pack(f, _):
        rows = pl.ds(pl.multiple_of(f * Q, Q), Q)
        low = jnp.zeros((Q, EY), F32)
        high = jnp.zeros((Q, EY), F32)
        for j in range(EX):
            values = u_ref[rows, block(j)]
            low = jnp.where(lane64 == j, pltpu.roll(values, j, 1) if j else values, low)
            high = jnp.where(lane64 == j, pltpu.roll(values, j + 1, 1), high)
        packed[0, rows, :] = low
        packed[1, rows, :] = high
        return 0

    for load in loads + lists:
        load.wait()
    lax.fori_loop(0, F, pack, 0)
    fold(inverse_ref, [own_ref[s] for s in range(4)] + [next_ref[s] for s in range(4)], g_ref)
    fold(inverse_ref, [project_ref[k] for k in range(4)], p_ref)
    pl.semaphore_wait(barrier, len(partners))
    for p in range(3):
        for s in range(4):
            side_copy(p, s).start()

    def interior(f, _):
        rows = pl.ds(pl.multiple_of(f * Q, Q), Q)
        u = u_ref[rows, :]
        made = product(g_ref[...], u)
        for j in range(EX):
            total = u[:, block(j)]
            for s in range(4):
                outward = jnp.maximum(v_ref[s, j : j + 1, :], 0.0)
                total = total - outward * made[s * Q : (s + 1) * Q, block(j)]
            inward = [jnp.minimum(v_ref[s, j : j + 1, :], 0.0) for s in range(4)]
            if j > 0:
                total = total - inward[0] * made[4 * Q : 5 * Q, block(j - 1)]
            if j < EX - 1:
                total = total - inward[1] * made[5 * Q : 6 * Q, block(j + 1)]
            before = pltpu.roll(made[6 * Q : 7 * Q, block(j)], 1, 1)
            after = pltpu.roll(made[7 * Q : 8 * Q, block(j)], EY - 1, 1)
            total = total - jnp.where(lane64 == 0, 0.0, inward[2] * before)
            total = total - jnp.where(lane64 == EY - 1, 0.0, inward[3] * after)
            lim_ref[rows, block(j)] = total
        return 0

    lax.fori_loop(0, F, interior, 0)

    def edges(p):
        first, count, _ = PARTS[p]
        for s in range(4):
            side_copy(p, s).wait_recv()

        def field(f, found):
            found = list(found)
            rows = pl.ds(pl.multiple_of((first + f) * Q, Q), Q)
            made = [
                product(g_ref[(4 + s) * Q : (5 + s) * Q, :], sides[s, rows, :]) for s in range(4)
            ]
            for j in range(EX):
                inward = [jnp.minimum(v_ref[s, j : j + 1, :], 0.0) * gate[s] for s in range(4)]
                total = lim_ref[rows, block(j)]
                if j == 0:
                    total = total - inward[0] * made[0]
                if j == EX - 1:
                    total = total - inward[1] * made[1]
                before = made[2] if j == 0 else pltpu.roll(made[2], EY - j, 1)
                after = pltpu.roll(made[3], EY - 1 - j, 1)
                total = total - jnp.where(lane64 == 0, inward[2] * before, 0.0)
                total = total - jnp.where(lane64 == EY - 1, inward[3] * after, 0.0)
                lim_ref[rows, block(j)] = total
                mean = jnp.sum(total, axis=0, keepdims=True) * (1.0 / Q)
                found[j] = jnp.where(row8 == f, mean, found[j])
            return tuple(found)

        found = lax.fori_loop(
            0, count, field, tuple(jnp.zeros((8, EY), F32) for _ in range(EX))
        )
        low = jnp.zeros((8, EY), F32)
        high = jnp.zeros((8, EY), F32)
        for j in range(EX):
            means[p, :, block(j)] = found[j]
            low = jnp.where(lane8 == j, pltpu.roll(found[j], j, 1) if j else found[j], low)
            high = jnp.where(lane8 == j, pltpu.roll(found[j], j + 1, 1), high)
        mean_packed[p, 0] = low
        mean_packed[p, 1] = high
        for s in range(4):
            mean_copy(p, s).start()

    def limit(p):
        first, count, _ = PARTS[p]
        for s in range(4):
            mean_copy(p, s).wait_recv()
        for j in range(EX):
            center = means[p, :, block(j)]
            if j > 0:
                left = means[p, :, block(j - 1)]
            else:
                left = jnp.where(gate[0] > 0, mean_sides[p, 0], center)
            if j < EX - 1:
                right = means[p, :, block(j + 1)]
            else:
                right = jnp.where(gate[1] > 0, mean_sides[p, 1], center)
            before = mean_sides[p, 2] if j == 0 else pltpu.roll(mean_sides[p, 2], EY - j, 1)
            before = jnp.where(gate[2] > 0, before, center)
            before = jnp.where(lane8 == 0, before, pltpu.roll(center, 1, 1))
            after = pltpu.roll(mean_sides[p, 3], EY - 1 - j, 1)
            after = jnp.where(gate[3] > 0, after, center)
            after = jnp.where(lane8 == EY - 1, after, pltpu.roll(center, EY - 1, 1))
            lower, upper = center, center
            for other in (left, right, before, after):
                lower = jnp.minimum(lower, other)
                upper = jnp.maximum(upper, other)
            lower, upper = lower - MARGIN, upper + MARGIN
            for f in range(count):
                rows = slice((first + f) * Q, (first + f + 1) * Q)
                values = jnp.maximum(lim_ref[rows, block(j)], lower[f : f + 1])
                lim_ref[rows, block(j)] = jnp.minimum(values, upper[f : f + 1])
        states_copy(p, 1, 0).start()
        states_copy(p, 3, 1).start()

    for p in range(3):
        edges(p)
    for p in range(3):
        limit(p)

    table = rank_table(owner_ref, slot_ref, weight_ref)
    for p in range(3):
        states_copy(p, 1, 1).start()
        states_copy(p, 3, 0).start()
    for p in range(3):
        axes = PARTS[p][2]
        part_table(table, axes, tables[p])
        at[p][0] = tables[p][here[axes[0]]]
        for d in (2, 1, 3):
            table_copy(p, d).start()
    for p in range(3):
        for d in (1, 3):
            states_copy(p, d, d // 2).wait_recv()
            relay_copy(p, d).start()

    element = lax.broadcasted_iota(jnp.int32, (E, 256), 0).astype(F32)
    quarter = lax.rem(lax.broadcasted_iota(jnp.int32, (1, 256), 1) // CAP, 4)

    split, picked = (sp0, sp1, sp2), (pk0, pk1, pk2)

    def cut(p, d):
        first, count, _ = PARTS[p]
        rows = count * Q
        if d == 2:
            relay_copy(p, 1).wait_recv()
            relay_copy(p, 3).wait_recv()
        elif d:
            states_copy(p, d, 1 - d // 2).wait_recv()
        values = lim_ref[first * Q : first * Q + rows, :] if d == 0 else ar[p][3 - d]
        high, low = halves(values)
        split[p][(4 - d) % 4, 0:rows, :] = high
        split[p][(4 - d) % 4, rows : 2 * rows, :] = low

    def info_of(p, d, j, what):
        group = lax.rem(here[PARTS[p][2][1]] + d, 4) * 2
        tile = at[p][j, what]
        lanes = []
        for core in range(2):
            row = jnp.where(row8 == group + core, tile, 0.0)
            row = jnp.sum(row, axis=0, keepdims=True)
            lanes.append(pltpu.roll(row, CAP * j, 1) if j else row)
        return jnp.concatenate(lanes, axis=1)

    def pick(p, d, j):
        rows = PARTS[p][1] * Q
        hot = jnp.where(element == info_of(p, d, j, 0), 1.0, 0.0).astype(BF16)
        made = jnp.dot(split[p][j], hot, preferred_element_type=F32)
        picked[p][j] = made[0:rows] + made[rows:]

    def route(p, d):
        _, count, axes = PARTS[p]
        rows = count * Q
        infos = [[info_of(p, d, j, what) for what in (1, 2, 3)] for j in range(4)]
        slots = jnp.zeros((8, 256), F32)
        for o in range(4):
            which, slot, weight = infos[3]
            for j in range(3):
                mine = quarter == (o + j) % 4
                which = jnp.where(mine, infos[j][0], which)
                slot = jnp.where(mine, infos[j][1], slot)
                weight = jnp.where(mine, infos[j][2], weight)
            for f in range(count):
                part = slice(f * Q, (f + 1) * Q)
                values = picked[p][3, part, :]
                for j in range(3):
                    values = jnp.where(quarter == (o + j) % 4, picked[p][j, part, :], values)
                made = product(p_ref[...], values)
                chosen = made[3 * Q :]
                for k in range(3):
                    chosen = jnp.where(which == float(k), made[k * Q : (k + 1) * Q], chosen)
                chosen = chosen * weight
                place = slice(o * rows + f * Q, o * rows + (f + 1) * Q)
                bs[p][d, 0, place, :] = chosen[:, 0:128]
                bs[p][d, 1, place, :] = chosen[:, 128:256]
            slots = jnp.where(row256 == o, slot, slots)
        bs[p][d, 0, 4 * rows : 4 * rows + 8, :] = slots[:, 0:128]
        bs[p][d, 1, 4 * rows : 4 * rows + 8, :] = slots[:, 128:256]
        block_copy(p, d, 1).start()

        if isinstance(d, int):
            block_copy(p, d, 0).start()
        else:

            @pl.when(d > 0)
            def _():
                block_copy(p, d, 0).start()


    def landed(p, number):
        d = (0, 1, 3, 2)[number]
        if d == 0:
            own_copy(p).wait()
        else:
            block_copy(p, d, 0).wait_recv()
        block_copy(p, d, 1).wait_recv()

    def arrived(p, number, distance):
        _, count, axes = PARTS[p]
        rows = count * Q
        slot_of = (0, 3, 1, 2)[number]
        o = lax.rem(here[axes[2]] + distance, 4)
        place = pl.ds(pl.multiple_of(o * rows, rows), rows)
        high, low = halves(br[p][slot_of, place, :])
        pair[0:rows, :] = high
        pair[rows : 2 * rows, :] = low
        slot = br[p][slot_of, 4 * rows : 4 * rows + 8, :]
        slot = jnp.sum(jnp.where(row256 == o, slot, 0.0), axis=0, keepdims=True)
        hot = jnp.where(element == slot, 1.0, 0.0)
        made = lax.dot_general(
            pair[0 : 2 * rows, :],
            hot.astype(BF16),
            (((1,), (1,)), ((), ())),
            preferred_element_type=F32,
        )
        total = made[0:rows] + made[rows:]
        if number > 0:
            total = total + cs[p][o]
        cs[p][o] = total

    def gather(p, number):
        landed(p, number)

        def step(distance, _):
            arrived(p, number, distance)
            return 0

        lax.fori_loop(0, 4, step, 0)

    def gather_last(ps):
        for distance in (2, 1, 3, 0):
            for p in ps:
                if distance == 2:
                    landed(p, 3)
                arrived(p, 3, distance)
                if distance == 2:
                    far_sum(p, 1).start()
                    far_sum(p, 3).start()
        for p in ps:
            near_sum(p, 1, 1).start()
            near_sum(p, 3, 0).start()

    def combine(p):
        half = PARTS[p][1] * Q // 2
        for d in (1, 3):
            far_sum(p, d).wait_recv()
            o = owner_at(p, d)
            place = slice((d // 2) * half, (d // 2 + 1) * half)
            cs[p][o, place, :] = cs[p][o, place, :] + ct[p][d // 2]
            near_sum(p, d, d // 2).start()

    def finish(p):
        for h in (0, 1):
            near_sum(p, 1, h).wait_recv()
            near_sum(p, 3, h).wait_recv()
        out[p][...] = cs[p][owner_at(p, 0)] + cr[p][0] + cr[p][1]

    for d in (0, 1, 3):
        for p in range(3):
            cut(p, d)
    for p in range(3):
        for d in (1, 2, 3):
            table_copy(p, d).wait_recv()
    for p in range(3):
        for j in (0, 1, 3):
            pick(p, 2, j)
    for p in range(3):
        cut(p, 2)
        pick(p, 2, 2)
        route(p, 2)

    def towards(step, _):
        d = lax.rem(6 - step + (step // 2) * (2 * step - 1), 4)
        for p in range(3):
            for j in range(4):
                pick(p, d, j)
            route(p, d)
        return 0

    lax.fori_loop(1, 4, towards, 0)
    for p in range(3):
        own_copy(p).start()
    for p in (2, 0, 1):
        gather(p, 0)
    gather(2, 1)
    gather(2, 2)
    for number in (1, 2):
        gather(0, number)
        gather(1, number)
    gather_last((0, 1, 2))
    for p in (0, 1, 2):
        combine(p)
    for p in (0, 1, 2):
        finish(p)
    for p in range(3):
        for s in range(4):
            side_copy(p, s).wait_send()
            mean_copy(p, s).wait_send()
        for d in (1, 3):
            for h in (0, 1):
                states_copy(p, d, h).wait_send()
                near_sum(p, d, h).wait_send()
            relay_copy(p, d).wait_send()
            far_sum(p, d).wait_send()
        for d in (1, 2, 3):
            table_copy(p, d).wait_send()
            block_copy(p, d, 0).wait_send()
            block_copy(p, d, 1).wait_send()
        block_copy(p, 0, 1).wait_send()


def body(
    states,
    swept_volume,
    flux_own,
    flux_next,
    mass_inverse,
    projection,
    new_owner,
    new_slot,
    intersection_weight,
):
    rows = [count * Q for _, count, _ in PARTS]
    dma = pltpu.SemaphoreType.DMA
    made = pl.pallas_call(
        kernel,
        out_shape=[jax.ShapeDtypeStruct((r, E), F32) for r in rows],
        in_specs=[pl.BlockSpec(memory_space=pl.ANY)] + [VMEM] * 5 + [HBM] * 3,
        out_specs=[VMEM] * 3,
        scratch_shapes=[
            pltpu.VMEM((K, E), jnp.int32),
            pltpu.VMEM((K, E), jnp.int32),
            pltpu.VMEM((K, E), F32),
            pltpu.VMEM((COLS, E), F32),
            pltpu.VMEM((8 * Q, 3 * Q), BF16),
            pltpu.VMEM((4 * Q, 3 * Q), BF16),
            pltpu.VMEM((COLS, E), F32),
            pltpu.VMEM((4, COLS, EY), F32),
            pltpu.VMEM((2, COLS, EY), F32),
            pltpu.VMEM((3, 8, E), F32),
            pltpu.VMEM((3, 4, 8, EY), F32),
            pltpu.VMEM((3, 2, 8, EY), F32),
        ]
        + [pltpu.VMEM((4, 4, 8, 128), F32) for r in rows]
        + [pltpu.VMEM((3, r, E), F32) for r in rows]
        + [pltpu.VMEM((4, 4, 8, 128), F32) for r in rows]
        + [pltpu.VMEM((4, 2, 4 * r + 8, 128), F32) for r in rows]
        + [pltpu.VMEM((4, 4 * r + 8, 256), F32) for r in rows]
        + [pltpu.VMEM((4, r, E), F32) for r in rows]
        + [pltpu.VMEM((2, r, E), F32) for r in rows]
        + [pltpu.VMEM((2, r // 2, E), F32) for r in rows]
        + [
            *[pltpu.VMEM((4, 2 * r, E), BF16) for r in rows],
            *[pltpu.VMEM((4, r, 256), F32) for r in rows],
            pltpu.VMEM((2 * max(rows), 256), BF16),
            dma((EX + 3,)),
            *[dma((3, 4))] * 4,
            *[dma((3, 2, 2))] * 2,
            *[dma((3, 2))] * 2,
            *[dma((3, 3))] * 2,
            *[dma((3, 4, 2))] * 2,
            *[dma((3, 2, 2))] * 2,
            *[dma((3, 2))] * 2,
            dma((3,)),
        ],
        compiler_params=pltpu.CompilerParams(
            collective_id=0, has_side_effects=True, vmem_limit_bytes=56 * 2**20
        ),
    )(
        states.reshape(COLS, EX, EY),
        swept_volume,
        mass_inverse,
        flux_own,
        flux_next,
        projection,
        new_owner.reshape(E, K).T,
        new_slot.reshape(E, K).T,
        intersection_weight.reshape(E, K).T,
    )
    return jnp.concatenate(made, axis=0).reshape(F, Q, E)


def solution(mesh):
    placed = (
        P(None, None, "gx", "gy"),
        P(None, "gx", "gy"),
        P(),
        P(),
        P(),
        P(),
        P("gx", "gy", None, None),
        P("gx", "gy", None, None),
        P("gx", "gy", None, None),
    )
    return jax.shard_map(
        body, mesh=mesh, in_specs=placed, out_specs=P(None, None, ("gx", "gy")), check_vma=False
    )
```

```python
import functools

import jax
import jax.numpy as jnp
from jax import lax
from jax.experimental import pallas as pl
from jax.experimental.pallas import tpu as pltpu
from jax.sharding import PartitionSpec as P

F, Q, K, EX, EY, CAP = 8, 64, 4, 4, 128, 32
E = EX * EY
COLS = F * Q
MARGIN = 0.75
MESH = pl.DeviceIdType.MESH
VMEM = pl.BlockSpec(memory_space=pltpu.VMEM)
HBM = pl.BlockSpec(memory_space=pltpu.HBM)
F32, BF16 = jnp.float32, jnp.bfloat16
PARTS = ((0, 3, "xyz"), (3, 3, "yzx"), (6, 2, "zxy"))


def halves(values):
    high = values.astype(BF16)
    return high, (values - high.astype(F32)).astype(BF16)


def product(matrix, values):
    high, low = halves(values)
    stacked = jnp.concatenate([high, low, high], axis=0)
    return jnp.dot(matrix, stacked, preferred_element_type=F32)


def fold(inverse_ref, sources, target_ref):
    inverse = inverse_ref[...]
    for term, source in enumerate(sources):
        made = jnp.dot(
            inverse, source, precision=lax.Precision.HIGHEST, preferred_element_type=F32
        )
        high, low = halves(made)
        target_ref[term * Q : (term + 1) * Q, :] = jnp.concatenate([high, high, low], axis=1)


def rank_table(owner_ref, slot_ref, weight_ref):
    devices = lax.broadcasted_iota(jnp.int32, (128, 256), 0)
    ranks = lax.broadcasted_iota(jnp.int32, (CAP, 256), 0).astype(F32)
    earlier = lax.broadcasted_iota(jnp.int32, (256, 256), 0) < lax.broadcasted_iota(
        jnp.int32, (256, 256), 1
    )
    earlier = jnp.where(earlier, 1.0, 0.0).astype(BF16)
    carry = jnp.zeros((128, 1), F32)
    table = jnp.zeros((128, 8 * CAP), F32)
    for k in range(K):
        for start in range(0, E, 256):
            lanes = slice(start, start + 256)
            named = jnp.where(devices == owner_ref[k : k + 1, lanes], 1.0, 0.0)
            before = jnp.dot(named.astype(BF16), earlier, preferred_element_type=F32) + carry
            rank = jnp.sum(named * before, axis=0, keepdims=True)
            carry = carry + jnp.sum(named, axis=1, keepdims=True)
            placed = ranks == rank
            weight = weight_ref[k : k + 1, lanes]
            first = weight.astype(BF16).astype(F32)
            second = (weight - first).astype(BF16).astype(F32)
            slot = slot_ref[k : k + 1, lanes]
            element = lax.broadcasted_iota(jnp.int32, (1, 256), 1) + (start + 1)
            parts = [
                (element // 128).astype(F32),
                lax.rem(element, 128).astype(F32),
                jnp.full((1, 256), float(k), F32),
                (slot // 128).astype(F32),
                lax.rem(slot, 128).astype(F32),
                first,
                second,
                weight - first - second,
            ]
            values = jnp.concatenate([jnp.where(placed, row, 0.0) for row in parts], axis=0)
            table = table + lax.dot_general(
                named.astype(BF16),
                values.astype(BF16),
                (((1,), (1,)), ((), ())),
                preferred_element_type=F32,
            )
    return table.astype(BF16)


STRIDE = {"z": 32, "y": 8, "x": 2}


def part_table(table, axes, target_ref):
    a, b, c = axes
    row = lax.broadcasted_iota(jnp.int32, (32, 128), 0)
    lane = lax.broadcasted_iota(jnp.int32, (32, 128), 1)
    first = (row // 8) * STRIDE[a] + lax.rem(row // 2, 4) * STRIDE[b] + lax.rem(row, 2)
    quarter = lane // CAP
    made = [jnp.zeros((32, 128), F32)] * 8
    for o in range(4):
        chosen = jnp.where(lane == first + o * STRIDE[c], 1.0, 0.0).astype(BF16)
        found = jnp.dot(chosen, table, preferred_element_type=F32)
        for m in range(8):
            tile = found[:, (m // 4) * 128 : (m // 4 + 1) * 128]
            turn = (o - m % 4) % 4
            tile = pltpu.roll(tile, turn * CAP, 1) if turn else tile
            made[m] = jnp.where(quarter == o, tile, made[m])
    whats = (
        made[0] * 128 + made[1] - 1,
        made[2],
        made[3] * 128 + made[4],
        made[5] + made[6] + made[7],
    )
    for place in range(4):
        for number, what in enumerate(whats):
            target_ref[place, number] = what[place * 8 : (place + 1) * 8]


def kernel(
    states_ref, v_ref, inverse_ref, own_ref, next_ref, project_ref,
    owner_hbm, slot_hbm, weight_hbm, out0, out1, out2, owner_ref, slot_ref, weight_ref, u_ref, g_ref, p_ref, lim_ref, sides, packed, means, mean_sides, mean_packed,
    tb0, tb1, tb2, ar0, ar1, ar2, at0, at1, at2, bs0, bs1, bs2, br0, br1, br2,
    cs0, cs1, cs2, cr0, cr1, cr2, ct0, ct1, ct2, sp0, sp1, sp2, pk0, pk1, pk2, pair,
    u_sem, h_send, h_recv, m_send, m_recv,
    a_send, a_recv, f_send, f_recv, t_send, t_recv, b_send, b_recv, c_send, c_recv, d_send, d_recv,
    own_sem,
):
    tables, ar, at = (tb0, tb1, tb2), (ar0, ar1, ar2), (at0, at1, at2)
    bs, br, cs, cr = (bs0, bs1, bs2), (br0, br1, br2), (cs0, cs1, cs2), (cr0, cr1, cr2)
    ct, out = (ct0, ct1, ct2), (out0, out1, out2)
    gx, gy = lax.axis_index("gx"), lax.axis_index("gy")
    n_x, n_y = lax.axis_size("gx"), lax.axis_size("gy")
    here = {"x": gy // 2, "y": lax.rem(gx, 4), "z": gx // 4, "c": lax.rem(gy, 2)}
    near = (
        (lax.rem(gx + n_x - 1, n_x), gy),
        (lax.rem(gx + 1, n_x), gy),
        (gx, lax.rem(gy + n_y - 1, n_y)),
        (gx, lax.rem(gy + 1, n_y)),
    )
    inside = (gx > 0, gx < n_x - 1, gy > 0, gy < n_y - 1)
    gate = [jnp.where(there, 1.0, 0.0).astype(F32) for there in inside]

    def away(axis, distance, core=0):
        at_ = dict(here)
        at_[axis] = lax.rem(here[axis] + distance, 4)
        at_["c"] = lax.rem(here["c"] + core, 2)
        return (at_["z"] * 4 + at_["y"], at_["x"] * 2 + at_["c"])

    partners = [away(axis, d, core) for axis in "xyz" for d in (1, 2, 3) for core in (0, 1)]
    partners += [away("x", 0, 1), *near[:2]]
    loads = [
        pltpu.make_async_copy(
            states_ref.at[:, j, :], u_ref.at[:, pl.ds(j * EY, EY)], u_sem.at[j]
        )
        for j in range(EX)
    ]
    lists = [
        pltpu.make_async_copy(source, target, u_sem.at[EX + i])
        for i, (source, target) in enumerate(
            ((owner_hbm, owner_ref), (slot_hbm, slot_ref), (weight_hbm, weight_ref))
        )
    ]
    for load in loads + lists:
        load.start()
    barrier = pltpu.get_barrier_semaphore()
    for device in partners:
        pl.semaphore_signal(barrier, inc=1, device_id=device, device_id_type=MESH)

    def remote(source, target, send, recv, device):
        return pltpu.make_async_remote_copy(
            src_ref=source,
            dst_ref=target,
            send_sem=send,
            recv_sem=recv,
            device_id=device,
            device_id_type=MESH,
        )

    def rows_of(p):
        first, count, _ = PARTS[p]
        return pl.ds(first * Q, count * Q)

    def side_copy(p, s):
        rows = rows_of(p)
        source = (
            u_ref.at[rows, pl.ds(0, EY)],
            u_ref.at[rows, pl.ds(3 * EY, EY)],
            packed.at[0, rows],
            packed.at[1, rows],
        )[s]
        return remote(
            source, sides.at[s ^ 1, rows], h_send.at[p, s], h_recv.at[p, s ^ 1], near[s]
        )

    def mean_copy(p, s):
        source = (
            means.at[p, :, pl.ds(0, EY)],
            means.at[p, :, pl.ds(3 * EY, EY)],
            mean_packed.at[p, 0],
            mean_packed.at[p, 1],
        )[s]
        return remote(
            source, mean_sides.at[p, s ^ 1], m_send.at[p, s], m_recv.at[p, s ^ 1], near[s]
        )

    def half_of(p, h):
        size = PARTS[p][1] * Q // 2
        return pl.ds(h * size, size)

    def states_copy(p, d, h):
        first, count, axes = PARTS[p]
        size = count * Q // 2
        return remote(
            lim_ref.at[pl.ds(first * Q + h * size, size)],
            ar[p].at[3 - d, half_of(p, h)],
            a_send.at[p, d // 2, h],
            a_recv.at[p, d // 2, h],
            away(axes[0], d),
        )

    def relay_copy(p, d):
        half = half_of(p, d // 2)
        return remote(
            ar[p].at[3 - d, half],
            ar[p].at[1, half],
            f_send.at[p, d // 2],
            f_recv.at[p, d // 2],
            away(PARTS[p][2][0], d),
        )

    def table_copy(p, d):
        axis = PARTS[p][2][0]
        return remote(
            tables[p].at[lax.rem(here[axis] + d, 4)],
            at[p].at[4 - d],
            t_send.at[p, d - 1],
            t_recv.at[p, d - 1],
            away(axis, d),
        )

    def block_copy(p, d, core):
        return remote(
            bs[p].at[d, lax.rem(here["c"] + core, 2)],
            br[p].at[lax.rem(4 - d, 4), :, pl.ds(core * 128, 128)],
            b_send.at[p, d, core],
            b_recv.at[p, d, core],
            away(PARTS[p][2][1], d, core),
        )

    def own_copy(p):
        return pltpu.make_async_copy(
            bs[p].at[0, here["c"]], br[p].at[0, :, pl.ds(0, 128)], own_sem.at[p]
        )

    def owner_at(p, d):
        return lax.rem(here[PARTS[p][2][2]] + d, 4)

    def far_sum(p, d):
        return remote(
            cs[p].at[owner_at(p, 2), half_of(p, d // 2)],
            ct[p].at[d // 2],
            d_send.at[p, d // 2],
            d_recv.at[p, d // 2],
            away(PARTS[p][2][2], d),
        )

    def near_sum(p, d, h):
        half = half_of(p, h)
        return remote(
            cs[p].at[owner_at(p, d), half],
            cr[p].at[d // 2, half],
            c_send.at[p, d // 2, h],
            c_recv.at[p, d // 2, h],
            away(PARTS[p][2][2], d),
        )

    lane64 = lax.broadcasted_iota(jnp.int32, (Q, EY), 1)
    lane8 = lax.broadcasted_iota(jnp.int32, (8, EY), 1)
    row8 = lax.broadcasted_iota(jnp.int32, (8, EY), 0)
    row256 = lax.broadcasted_iota(jnp.int32, (8, 256), 0)

    def block(j):
        return slice(j * EY, (j + 1) * EY)

    def pack(f, _):
        rows = pl.ds(pl.multiple_of(f * Q, Q), Q)
        low = jnp.zeros((Q, EY), F32)
        high = jnp.zeros((Q, EY), F32)
        for j in range(EX):
            values = u_ref[rows, block(j)]
            low = jnp.where(lane64 == j, pltpu.roll(values, j, 1) if j else values, low)
            high = jnp.where(lane64 == j, pltpu.roll(values, j + 1, 1), high)
        packed[0, rows, :] = low
        packed[1, rows, :] = high
        return 0

    for load in loads + lists:
        load.wait()
    lax.fori_loop(0, F, pack, 0)
    fold(inverse_ref, [own_ref[s] for s in range(4)] + [next_ref[s] for s in range(4)], g_ref)
    pl.semaphore_wait(barrier, len(partners))
    for p in range(3):
        for s in range(4):
            side_copy(p, s).start()

    def interior(f, _):
        rows = pl.ds(pl.multiple_of(f * Q, Q), Q)
        u = u_ref[rows, :]
        made = product(g_ref[...], u)
        for j in range(EX):
            total = u[:, block(j)]
            for s in range(4):
                outward = jnp.maximum(v_ref[s, j : j + 1, :], 0.0)
                total = total - outward * made[s * Q : (s + 1) * Q, block(j)]
            inward = [jnp.minimum(v_ref[s, j : j + 1, :], 0.0) for s in range(4)]
            if j > 0:
                total = total - inward[0] * made[4 * Q : 5 * Q, block(j - 1)]
            if j < EX - 1:
                total = total - inward[1] * made[5 * Q : 6 * Q, block(j + 1)]
            before = pltpu.roll(made[6 * Q : 7 * Q, block(j)], 1, 1)
            after = pltpu.roll(made[7 * Q : 8 * Q, block(j)], EY - 1, 1)
            total = total - jnp.where(lane64 == 0, 0.0, inward[2] * before)
            total = total - jnp.where(lane64 == EY - 1, 0.0, inward[3] * after)
            lim_ref[rows, block(j)] = total
        return 0

    lax.fori_loop(0, F, interior, 0)

    def edges(p):
        first, count, _ = PARTS[p]
        for s in range(4):
            side_copy(p, s).wait_recv()

        def field(f, found):
            found = list(found)
            rows = pl.ds(pl.multiple_of((first + f) * Q, Q), Q)
            made = [
                product(g_ref[(4 + s) * Q : (5 + s) * Q, :], sides[s, rows, :]) for s in range(4)
            ]
            for j in range(EX):
                inward = [jnp.minimum(v_ref[s, j : j + 1, :], 0.0) * gate[s] for s in range(4)]
                total = lim_ref[rows, block(j)]
                if j == 0:
                    total = total - inward[0] * made[0]
                if j == EX - 1:
                    total = total - inward[1] * made[1]
                before = made[2] if j == 0 else pltpu.roll(made[2], EY - j, 1)
                after = pltpu.roll(made[3], EY - 1 - j, 1)
                total = total - jnp.where(lane64 == 0, inward[2] * before, 0.0)
                total = total - jnp.where(lane64 == EY - 1, inward[3] * after, 0.0)
                lim_ref[rows, block(j)] = total
                mean = jnp.sum(total, axis=0, keepdims=True) * (1.0 / Q)
                found[j] = jnp.where(row8 == f, mean, found[j])
            return tuple(found)

        found = lax.fori_loop(
            0, count, field, tuple(jnp.zeros((8, EY), F32) for _ in range(EX))
        )
        low = jnp.zeros((8, EY), F32)
        high = jnp.zeros((8, EY), F32)
        for j in range(EX):
            means[p, :, block(j)] = found[j]
            low = jnp.where(lane8 == j, pltpu.roll(found[j], j, 1) if j else found[j], low)
            high = jnp.where(lane8 == j, pltpu.roll(found[j], j + 1, 1), high)
        mean_packed[p, 0] = low
        mean_packed[p, 1] = high
        for s in range(4):
            mean_copy(p, s).start()

    def limit(p):
        first, count, _ = PARTS[p]
        for s in range(4):
            mean_copy(p, s).wait_recv()
        for j in range(EX):
            center = means[p, :, block(j)]
            if j > 0:
                left = means[p, :, block(j - 1)]
            else:
                left = jnp.where(gate[0] > 0, mean_sides[p, 0], center)
            if j < EX - 1:
                right = means[p, :, block(j + 1)]
            else:
                right = jnp.where(gate[1] > 0, mean_sides[p, 1], center)
            before = mean_sides[p, 2] if j == 0 else pltpu.roll(mean_sides[p, 2], EY - j, 1)
            before = jnp.where(gate[2] > 0, before, center)
            before = jnp.where(lane8 == 0, before, pltpu.roll(center, 1, 1))
            after = pltpu.roll(mean_sides[p, 3], EY - 1 - j, 1)
            after = jnp.where(gate[3] > 0, after, center)
            after = jnp.where(lane8 == EY - 1, after, pltpu.roll(center, EY - 1, 1))
            lower, upper = center, center
            for other in (left, right, before, after):
                lower = jnp.minimum(lower, other)
                upper = jnp.maximum(upper, other)
            lower, upper = lower - MARGIN, upper + MARGIN
            for f in range(count):
                rows = slice((first + f) * Q, (first + f + 1) * Q)
                values = jnp.maximum(lim_ref[rows, block(j)], lower[f : f + 1])
                lim_ref[rows, block(j)] = jnp.minimum(values, upper[f : f + 1])
        states_copy(p, 1, 0).start()
        states_copy(p, 3, 1).start()

    for p in range(3):
        edges(p)
    for p in range(3):
        limit(p)

    fold(inverse_ref, [project_ref[k] for k in range(4)], p_ref)
    for p in range(3):
        states_copy(p, 1, 1).start()
        states_copy(p, 3, 0).start()
    table = rank_table(owner_ref, slot_ref, weight_ref)
    for p in range(3):
        axes = PARTS[p][2]
        part_table(table, axes, tables[p])
        at[p][0] = tables[p][here[axes[0]]]
        for d in (2, 1, 3):
            table_copy(p, d).start()
    for p in range(3):
        for d in (1, 3):
            states_copy(p, d, d // 2).wait_recv()
            relay_copy(p, d).start()

    element = lax.broadcasted_iota(jnp.int32, (E, 256), 0).astype(F32)
    quarter = lax.rem(lax.broadcasted_iota(jnp.int32, (1, 256), 1) // CAP, 4)

    split, picked = (sp0, sp1, sp2), (pk0, pk1, pk2)

    def cut(p, d):
        first, count, _ = PARTS[p]
        rows = count * Q
        if d == 2:
            relay_copy(p, 1).wait_recv()
            relay_copy(p, 3).wait_recv()
        elif d:
            states_copy(p, d, 1 - d // 2).wait_recv()
        values = lim_ref[first * Q : first * Q + rows, :] if d == 0 else ar[p][3 - d]
        high, low = halves(values)
        split[p][(4 - d) % 4, 0:rows, :] = high
        split[p][(4 - d) % 4, rows : 2 * rows, :] = low

    def info_of(p, d, j, what):
        group = lax.rem(here[PARTS[p][2][1]] + d, 4) * 2
        tile = at[p][j, what]
        lanes = []
        for core in range(2):
            row = jnp.where(row8 == group + core, tile, 0.0)
            row = jnp.sum(row, axis=0, keepdims=True)
            lanes.append(pltpu.roll(row, CAP * j, 1) if j else row)
        return jnp.concatenate(lanes, axis=1)

    def pick(p, d, j):
        rows = PARTS[p][1] * Q
        hot = jnp.where(element == info_of(p, d, j, 0), 1.0, 0.0).astype(BF16)
        made = jnp.dot(split[p][j], hot, preferred_element_type=F32)
        picked[p][j] = made[0:rows] + made[rows:]

    def route(p, d):
        _, count, axes = PARTS[p]
        rows = count * Q
        infos = [[info_of(p, d, j, what) for what in (1, 2, 3)] for j in range(4)]
        slots = jnp.zeros((8, 256), F32)
        for o in range(4):
            which, slot, weight = infos[3]
            for j in range(3):
                mine = quarter == (o + j) % 4
                which = jnp.where(mine, infos[j][0], which)
                slot = jnp.where(mine, infos[j][1], slot)
                weight = jnp.where(mine, infos[j][2], weight)
            for f in range(count):
                part = slice(f * Q, (f + 1) * Q)
                values = picked[p][3, part, :]
                for j in range(3):
                    values = jnp.where(quarter == (o + j) % 4, picked[p][j, part, :], values)
                made = product(p_ref[...], values)
                chosen = made[3 * Q :]
                for k in range(3):
                    chosen = jnp.where(which == float(k), made[k * Q : (k + 1) * Q], chosen)
                chosen = chosen * weight
                place = slice(o * rows + f * Q, o * rows + (f + 1) * Q)
                bs[p][d, 0, place, :] = chosen[:, 0:128]
                bs[p][d, 1, place, :] = chosen[:, 128:256]
            slots = jnp.where(row256 == o, slot, slots)
        bs[p][d, 0, 4 * rows : 4 * rows + 8, :] = slots[:, 0:128]
        bs[p][d, 1, 4 * rows : 4 * rows + 8, :] = slots[:, 128:256]
        block_copy(p, d, 1).start()

        if isinstance(d, int):
            block_copy(p, d, 0).start()
        else:

            @pl.when(d > 0)
            def _():
                block_copy(p, d, 0).start()


    def landed(p, number):
        d = (0, 1, 3, 2)[number]
        if d == 0:
            own_copy(p).wait()
        else:
            block_copy(p, d, 0).wait_recv()
        block_copy(p, d, 1).wait_recv()

    def arrived(p, number, distance):
        _, count, axes = PARTS[p]
        rows = count * Q
        slot_of = (0, 3, 1, 2)[number]
        o = lax.rem(here[axes[2]] + distance, 4)
        place = pl.ds(pl.multiple_of(o * rows, rows), rows)
        high, low = halves(br[p][slot_of, place, :])
        pair[0:rows, :] = high
        pair[rows : 2 * rows, :] = low
        slot = br[p][slot_of, 4 * rows : 4 * rows + 8, :]
        slot = jnp.sum(jnp.where(row256 == o, slot, 0.0), axis=0, keepdims=True)
        hot = jnp.where(element == slot, 1.0, 0.0)
        made = lax.dot_general(
            pair[0 : 2 * rows, :],
            hot.astype(BF16),
            (((1,), (1,)), ((), ())),
            preferred_element_type=F32,
        )
        total = made[0:rows] + made[rows:]
        if number > 0:
            total = total + cs[p][o]
        cs[p][o] = total

    def gather(p, number):
        landed(p, number)

        def step(distance, _):
            arrived(p, number, distance)
            return 0

        lax.fori_loop(0, 4, step, 0)

    def gather_last(ps):
        for distance in (2, 1, 3, 0):
            for p in ps:
                if distance == 2:
                    landed(p, 3)
                arrived(p, 3, distance)
                if distance == 2:
                    far_sum(p, 1).start()
                    far_sum(p, 3).start()
        for p in ps:
            near_sum(p, 1, 1).start()
            near_sum(p, 3, 0).start()

    def combine(p):
        half = PARTS[p][1] * Q // 2
        for d in (1, 3):
            far_sum(p, d).wait_recv()
            o = owner_at(p, d)
            place = slice((d // 2) * half, (d // 2 + 1) * half)
            cs[p][o, place, :] = cs[p][o, place, :] + ct[p][d // 2]
            near_sum(p, d, d // 2).start()

    def finish(p):
        for h in (0, 1):
            near_sum(p, 1, h).wait_recv()
            near_sum(p, 3, h).wait_recv()
        out[p][...] = cs[p][owner_at(p, 0)] + cr[p][0] + cr[p][1]

    for d in (0, 1, 3):
        for p in range(3):
            cut(p, d)
    for p in range(3):
        for d in (1, 2, 3):
            table_copy(p, d).wait_recv()
    for p in range(3):
        for j in (0, 1, 3):
            pick(p, 2, j)
    for p in range(3):
        cut(p, 2)
        pick(p, 2, 2)
        route(p, 2)

    def towards(step, _):
        d = lax.rem(6 - step + (step // 2) * (2 * step - 1), 4)
        for p in range(3):
            for j in range(4):
                pick(p, d, j)
            route(p, d)
        return 0

    lax.fori_loop(1, 4, towards, 0)
    for p in range(3):
        own_copy(p).start()
    for p in (2, 0, 1):
        gather(p, 0)
    gather(2, 1)
    gather(2, 2)
    for number in (1, 2):
        gather(0, number)
        gather(1, number)
    gather_last((0, 1, 2))
    for p in (0, 1, 2):
        combine(p)
    for p in (0, 1, 2):
        finish(p)
    for p in range(3):
        for s in range(4):
            side_copy(p, s).wait_send()
            mean_copy(p, s).wait_send()
        for d in (1, 3):
            for h in (0, 1):
                states_copy(p, d, h).wait_send()
                near_sum(p, d, h).wait_send()
            relay_copy(p, d).wait_send()
            far_sum(p, d).wait_send()
        for d in (1, 2, 3):
            table_copy(p, d).wait_send()
            block_copy(p, d, 0).wait_send()
            block_copy(p, d, 1).wait_send()
        block_copy(p, 0, 1).wait_send()


def body(
    states,
    swept_volume,
    flux_own,
    flux_next,
    mass_inverse,
    projection,
    new_owner,
    new_slot,
    intersection_weight,
):
    rows = [count * Q for _, count, _ in PARTS]
    dma = pltpu.SemaphoreType.DMA
    made = pl.pallas_call(
        kernel,
        out_shape=[jax.ShapeDtypeStruct((r, E), F32) for r in rows],
        in_specs=[pl.BlockSpec(memory_space=pl.ANY)] + [VMEM] * 5 + [HBM] * 3,
        out_specs=[VMEM] * 3,
        scratch_shapes=[
            pltpu.VMEM((K, E), jnp.int32),
            pltpu.VMEM((K, E), jnp.int32),
            pltpu.VMEM((K, E), F32),
            pltpu.VMEM((COLS, E), F32),
            pltpu.VMEM((8 * Q, 3 * Q), BF16),
            pltpu.VMEM((4 * Q, 3 * Q), BF16),
            pltpu.VMEM((COLS, E), F32),
            pltpu.VMEM((4, COLS, EY), F32),
            pltpu.VMEM((2, COLS, EY), F32),
            pltpu.VMEM((3, 8, E), F32),
            pltpu.VMEM((3, 4, 8, EY), F32),
            pltpu.VMEM((3, 2, 8, EY), F32),
        ]
        + [pltpu.VMEM((4, 4, 8, 128), F32) for r in rows]
        + [pltpu.VMEM((3, r, E), F32) for r in rows]
        + [pltpu.VMEM((4, 4, 8, 128), F32) for r in rows]
        + [pltpu.VMEM((4, 2, 4 * r + 8, 128), F32) for r in rows]
        + [pltpu.VMEM((4, 4 * r + 8, 256), F32) for r in rows]
        + [pltpu.VMEM((4, r, E), F32) for r in rows]
        + [pltpu.VMEM((2, r, E), F32) for r in rows]
        + [pltpu.VMEM((2, r // 2, E), F32) for r in rows]
        + [
            *[pltpu.VMEM((4, 2 * r, E), BF16) for r in rows],
            *[pltpu.VMEM((4, r, 256), F32) for r in rows],
            pltpu.VMEM((2 * max(rows), 256), BF16),
            dma((EX + 3,)),
            *[dma((3, 4))] * 4,
            *[dma((3, 2, 2))] * 2,
            *[dma((3, 2))] * 2,
            *[dma((3, 3))] * 2,
            *[dma((3, 4, 2))] * 2,
            *[dma((3, 2, 2))] * 2,
            *[dma((3, 2))] * 2,
            dma((3,)),
        ],
        compiler_params=pltpu.CompilerParams(
            collective_id=0, has_side_effects=True, vmem_limit_bytes=56 * 2**20
        ),
    )(
        states.reshape(COLS, EX, EY),
        swept_volume,
        mass_inverse,
        flux_own,
        flux_next,
        projection,
        new_owner.reshape(E, K).T,
        new_slot.reshape(E, K).T,
        intersection_weight.reshape(E, K).T,
    )
    return jnp.concatenate(made, axis=0).reshape(F, Q, E)


def solution(mesh):
    placed = (
        P(None, None, "gx", "gy"),
        P(None, "gx", "gy"),
        P(),
        P(),
        P(),
        P(),
        P("gx", "gy", None, None),
        P("gx", "gy", None, None),
        P("gx", "gy", None, None),
    )
    return jax.shard_map(
        body, mesh=mesh, in_specs=placed, out_specs=P(None, None, ("gx", "gy")), check_vma=False
    )
```
